32 devices in a mesh: batch: 4 (over y, x), tensor: 8 (over z, core).
Axes of the slice: x: 2, y: 2, z: 4, core: 2. Of those that a mesh axis runs over, the one named last changes fastest.
Arguments:
- hidden: bfloat16 [4096, 2048], P('batch', 'tensor'), may hold values from -6 to 6
- w_query: bfloat16 [2048, 2048], P(None, 'tensor'), may hold values from -0.125 to 0.125
- w_key: bfloat16 [2048, 2048], P(None, 'tensor'), may hold values from -0.125 to 0.125
- w_value: bfloat16 [2048, 4096], P(None, 'tensor'), may hold values from -0.125 to 0.125
- conv_query: float32 [4, 2048], P(None, 'tensor'), may hold values from -0.6 to 0.6
- conv_key: float32 [4, 2048], P(None, 'tensor'), may hold values from -0.6 to 0.6
- conv_value: float32 [4, 4096], P(None, 'tensor'), may hold values from -0.6 to 0.6
- decay_log: float32 [4096, 32], P('batch', 'tensor'), may hold values from -1 to 0, as said below
- beta_gate: float32 [4096, 32], P('batch', 'tensor'), may hold values from 0.1 to 0.95
- init_state: float32 [32, 32, 128, 128], P('batch', 'tensor'), may hold values from -4 to 4
- grad_out: bfloat16 [4096, 4096], P('batch', 'tensor'), may hold values from -6 to 6
- state_grad_in: float32 [32, 32, 128, 128], P('batch', 'tensor'), may hold values from -4 to 4
- rollout_lengths: int32 [32], P('batch'), may hold values from 1 to 128, 2560 in all
- slot_map: int32 [32], P('batch'), may hold values from 0 to 31, as said below
Outputs:
- grad_hidden: bfloat16 [4096, 2048], P('batch', 'tensor')
- grad_w_query: float32 [2048, 2048], P('batch', 'tensor')
- grad_w_key: float32 [2048, 2048], P('batch', 'tensor')
- grad_w_value: float32 [2048, 4096], P('batch', 'tensor')
- grad_conv_query: float32 [4, 2048], P(None, 'tensor')
- grad_conv_key: float32 [4, 2048], P(None, 'tensor')
- grad_conv_value: float32 [4, 4096], P(None, 'tensor')
- grad_decay: float32 [4096, 32], P('batch', 'tensor')
- grad_beta: float32 [4096, 32], P('batch', 'tensor')
- slot_state_grad: float32 [32, 32, 128, 128], P('batch', 'tensor')
The draws below stay inside these ranges and needn't reach their ends.
Inputs may be any that keep to these rules, and one draw needn't show every extreme that they name: `decay_log`: Non-positive. `slot_map`: each slot is named once; slot s is held by batch index s // 8; the 8 requests of one batch index go to 4 different slot holders, exactly 2 to each.
All inputs are finite; a program needn't handle non-finite values. No bound on the sum of `rollout_lengths` on one device may be relied on, other than what follows from the above.
Results may differ from the reference program's by a relative error of at most 0.014.
Values may be sent and summed in bfloat16 or wider, within the bound.
No kernel may reach another device: no remote copies, remote signals or barrier semaphores. Data moves between devices by JAX's collectives and lax.ppermute only.
A program may use at most 128 MiB of HBM per device.

```python
import math
import jax
import jax.numpy as jnp
import numpy as np
from jax import lax

D = 2048
KH = 16
VALUE_HEADS = 32
DK = 128
DV = 128
CONV = 4
WINDOW_LENGTH = 128
R_DEV = 8
CAP = 2
REQS = 32
TOTAL_ROWS = 4096
N_BATCH = 4
N_TENSOR = 8


def draw_decay_log(key, part):
    key = jax.random.fold_in(key, 11)
    frequency_key = jax.random.fold_in(key, 0)
    jitter_random_key = jax.random.fold_in(key, 3)
    spike_random_key = jax.random.fold_in(key, 4)
    length_random_key = jax.random.fold_in(key, 5)
    head_shape = (REQS, 1, VALUE_HEADS)
    baseline_rate = jnp.exp(jax.random.uniform(frequency_key, head_shape, minval=jnp.log(1.0 / (8.0 * WINDOW_LENGTH)), maxval=jnp.log(1.0 / 30.0)))
    draw_shape = (REQS, WINDOW_LENGTH, VALUE_HEADS)
    jitter_level = jax.random.uniform(jitter_random_key, draw_shape, minval=0.5, maxval=1.5)
    spike_matches = jax.random.bernoulli(spike_random_key, 3.0 / WINDOW_LENGTH, draw_shape)
    spike_events = jnp.where(spike_matches, jax.random.uniform(length_random_key, draw_shape, minval=0.22, maxval=0.7), 0.0)
    return (-(baseline_rate * jitter_level) - spike_events).reshape(TOTAL_ROWS, VALUE_HEADS).astype(jnp.float32)


def draw_slot_map(key, part):
    key = jax.random.fold_in(key, 5)
    shift_key, order_key, local_key = jax.random.split(key, 3)
    batch_count = REQS // R_DEV
    group_count = R_DEV // CAP
    shifts = jax.random.permutation(shift_key, batch_count)[:group_count]
    shuffled = jax.vmap(lambda sub_key: jax.random.permutation(sub_key, R_DEV))(jax.random.split(order_key, batch_count))
    device_ids = jnp.arange(batch_count, dtype=jnp.int32)[:, None]
    group_ids = shuffled // CAP
    within_group = shuffled % CAP
    owners = (device_ids + shifts[group_ids]) % batch_count
    local_slot = group_ids * CAP + within_group
    local_perm = jax.vmap(lambda sub_key: jax.random.permutation(sub_key, R_DEV))(jax.random.split(local_key, batch_count))
    slots = owners * R_DEV + local_perm[owners, local_slot]
    return slots.reshape(REQS).astype(jnp.int32)


def block_scale(rng, dims, cuts, least, high):
    factor_of, own = 1.0, jax.random.fold_in(rng, 6)
    for dim, blocks in cuts:
        heights = jnp.exp(jax.random.uniform(jax.random.fold_in(own, dim), (blocks,), jnp.float32, least / len(cuts), high / len(cuts)))
        factor_of = factor_of * jnp.repeat(heights, dims[dim] // blocks).reshape([-1 if axis == dim else 1 for axis in range(len(dims))])
    return factor_of


def split_up(amount, total, bound, skew):
    weights = [(1 << 20) // math.isqrt(rank ** skew) + 1 for rank in range(2, amount + 1)]
    spare, given = total - bound - (amount - 1), [1] * (amount - 1)
    while spare > 0:
        movable = [i for i in range(amount - 1) if given[i] < bound]
        pool, budget = sum([weights[i] for i in movable]), spare
        for i in movable:
            addition = min(bound - given[i], max(1, budget * weights[i] // pool), spare)
            given[i] = given[i] + addition
            spare = spare - addition
    return np.array([bound] + given)


def uneven_parts(own_key, number_of, total, reach, skew):
    if number_of == 2:
        one = jax.random.randint(own_key, (), max(1, total - reach), min(reach, total - 1) + 1)
        return jnp.stack([one, total - one])
    sizes = jnp.asarray(split_up(number_of, total, reach, skew), jnp.int32)
    couples = (number_of - 1) // 2
    donor, taker = sizes[1:1 + 2 * couples:2], sizes[2:2 + 2 * couples:2]
    margin = jnp.minimum(donor - 1, reach - taker)
    moved = jax.random.randint(jax.random.fold_in(own_key, 1), (couples,), 0, 1 << 20) % (margin + 1)
    sizes = sizes.at[1:1 + 2 * couples:2].set(donor - moved).at[2:2 + 2 * couples:2].set(taker + moved)
    return sizes[jax.random.permutation(jax.random.fold_in(own_key, 2), number_of)]


def gaussian(stream_key, dims, deviation, limit, cuts=(), kind=jnp.bfloat16):
    values = jax.random.normal(stream_key, dims, jnp.float32) * deviation
    if len(cuts) > 0:
        values = block_scale(stream_key, dims, cuts, -0.22, 0.18) * values
    return jnp.clip(values, min=-limit, max=limit).astype(kind)


def setup_inputs(seed: int = 0) -> dict:
    arg_keys = jax.random.split(jax.random.key(seed), 15)
    hidden = gaussian(arg_keys[0], (TOTAL_ROWS, D), 1.0, 6.0, ((0, 4), (1, 8)))
    w_query = gaussian(arg_keys[1], (D, KH * DK), D ** -0.5, 0.125, ((1, 8),))
    w_key = gaussian(arg_keys[2], (D, KH * DK), D ** -0.5, 0.125, ((1, 8),))
    w_value = gaussian(arg_keys[3], (D, VALUE_HEADS * DV), D ** -0.5, 0.125, ((1, 8),))
    conv_query = jnp.clip(jax.random.uniform(arg_keys[4], (CONV, KH * DK), jnp.float32, -0.6, 0.6) * block_scale(arg_keys[4], (CONV, KH * DK), ((1, 8),), -0.4, 0.0), -0.6, 0.6)
    conv_key = jnp.clip(jax.random.uniform(arg_keys[5], (CONV, KH * DK), jnp.float32, -0.6, 0.6) * block_scale(arg_keys[5], (CONV, KH * DK), ((1, 8),), -0.4, 0.0), -0.6, 0.6)
    conv_value = jnp.clip(jax.random.uniform(arg_keys[6], (CONV, VALUE_HEADS * DV), jnp.float32, -0.6, 0.6) * block_scale(arg_keys[6], (CONV, VALUE_HEADS * DV), ((1, 8),), -0.4, 0.0), -0.6, 0.6)
    decay_log = draw_decay_log(jax.random.fold_in(arg_keys[14], 71), 0)
    beta_gate = jnp.clip(0.1 + 0.84999999 * jax.random.uniform(arg_keys[8], (TOTAL_ROWS, VALUE_HEADS), jnp.float32) ** block_scale(arg_keys[8], (TOTAL_ROWS, VALUE_HEADS), ((0, 4), (1, 8)), -0.2, 0.2), 0.1, 0.95)
    init_state = gaussian(arg_keys[9], (REQS, VALUE_HEADS, DK, DV), 0.5, 4.0, ((0, 4), (1, 8)), jnp.float32)
    grad_out = gaussian(arg_keys[10], (TOTAL_ROWS, VALUE_HEADS * DV), 1.0, 6.0, ((0, 4), (1, 8)))
    state_grad_in = gaussian(arg_keys[11], (REQS, VALUE_HEADS, DK, DV), 0.5, 4.0, ((0, 4), (1, 8)), jnp.float32)
    rollout_lengths = uneven_parts(arg_keys[12], REQS, REQS * WINDOW_LENGTH * 5 // 8, WINDOW_LENGTH, 2).astype(jnp.int32)
    slot_map = draw_slot_map(jax.random.fold_in(arg_keys[14], 71), 0)
    return {"hidden": hidden, "w_query": w_query, "w_key": w_key, "w_value": w_value, "conv_query": conv_query, "conv_key": conv_key, "conv_value": conv_value, "decay_log": decay_log, "beta_gate": beta_gate, "init_state": init_state, "grad_out": grad_out, "state_grad_in": state_grad_in, "rollout_lengths": rollout_lengths, "slot_map": slot_map}


EPSILON = 1e-06

def short_conv(projected, weights):
    kernel_taps = weights.shape[0]
    length = projected.shape[1]
    padded = jnp.pad(projected, ((0, 0), (kernel_taps - 1, 0), (0, 0)))
    mixed_sum = jnp.zeros_like(projected)
    for offset in range(kernel_taps):
        mixed_sum = mixed_sum + padded[:, offset:offset + length, :] * weights[offset]
    return mixed_sum

def unit_rows(heads_in, factor):
    return heads_in * (factor * lax.rsqrt(lax.optimization_barrier(jnp.sum(heads_in * heads_in, axis=-1, keepdims=True)) + EPSILON))

def block_step(carry_state, blocks_in):
    queries, key_rows, values, gate_logs, write_rates = blocks_in
    precise = lax.Precision.HIGHEST
    block_len = gate_logs.shape[-1]
    cumulative = jnp.cumsum(gate_logs, axis=-1)
    row_index = lax.broadcasted_iota(jnp.int32, (block_len, block_len), 0)
    col_index = lax.broadcasted_iota(jnp.int32, (block_len, block_len), 1)
    strict = row_index > col_index
    causal = row_index >= col_index
    spread = cumulative[..., :, None] - cumulative[..., None, :]
    within = jnp.where(causal, jnp.exp(jnp.where(causal, spread, 0.0)), 0.0)
    intersections = jnp.einsum('rhik,rhjk->rhij', key_rows, key_rows, precision=precise)
    coupling = jnp.where(strict, write_rates[..., :, None] * intersections * within, 0.0)
    system = coupling + jnp.eye(block_len, dtype=jnp.float32)
    growth = jnp.exp(cumulative)
    weighted = (write_rates * growth)[..., None] * key_rows
    scaled = write_rates[..., None] * values
    solved_w = jax.scipy.linalg.solve_triangular(system, weighted, lower=True, unit_diagonal=True)
    solved_u = jax.scipy.linalg.solve_triangular(system, scaled, lower=True, unit_diagonal=True)
    new_values = solved_u - jnp.einsum('rhck,rhkv->rhcv', solved_w, carry_state, precision=precise)
    scores = jnp.einsum('rhik,rhjk->rhij', queries, key_rows, precision=precise) * within
    outputs = growth[..., None] * jnp.einsum('rhck,rhkv->rhcv', queries, carry_state, precision=precise)
    outputs = outputs + jnp.einsum('rhij,rhjv->rhiv', scores, new_values, precision=precise)
    final_gate = cumulative[..., -1:]
    carried = jnp.exp(final_gate - cumulative)[..., None] * key_rows
    new_state = jnp.exp(final_gate)[..., None] * carry_state
    new_state = new_state + jnp.einsum('rhck,rhcv->rhkv', carried, new_values, precision=precise)
    return (new_state, outputs)

def core(proj_query, proj_key, proj_value, conv_query, conv_key, conv_value, decay_log, beta_gate, init_state, live_rows):
    requests = init_state.shape[0]
    length = proj_query.shape[0] // requests
    head_count = init_state.shape[1]
    key_size = init_state.shape[2]
    value_size = init_state.shape[3]
    key_heads = proj_query.shape[1] // key_size
    group_size = head_count // key_heads
    block_len = min(length, 128)
    block_count = length // block_len

    def prepare(projected, weights):
        return jax.nn.silu(short_conv(projected.astype(jnp.float32).reshape(requests, length, -1), weights))
    queries = unit_rows(prepare(proj_query, conv_query).reshape(requests, length, key_heads, key_size), key_size ** (-0.5))
    key_rows = unit_rows(prepare(proj_key, conv_key).reshape(requests, length, key_heads, key_size), 1.0)
    values = prepare(proj_value, conv_value).reshape(requests, length, head_count, value_size)
    queries = jnp.repeat(queries, group_size, axis=2)
    key_rows = jnp.repeat(key_rows, group_size, axis=2)
    live_mask = live_rows.reshape(requests, length, 1)
    gate_logs = decay_log.reshape(requests, length, head_count) * live_mask
    write_rates = beta_gate.reshape(requests, length, head_count) * live_mask

    def to_blocks(array_in):
        dims_in = array_in.shape
        reshaped = array_in.reshape((requests, block_count, block_len) + dims_in[2:])
        return jnp.moveaxis(jnp.moveaxis(reshaped, 1, 0), 3, 2)
    final_state, outputs = lax.scan(block_step, init_state, (to_blocks(queries), to_blocks(key_rows), to_blocks(values), to_blocks(gate_logs), to_blocks(write_rates)))
    outputs = jnp.moveaxis(jnp.moveaxis(outputs, 0, 1), 2, 3)
    outputs = outputs.reshape(requests * length, head_count * value_size) * live_rows[:, None]
    return (outputs, final_state)

def core_grads(proj_query, proj_key, proj_value, conv_query, conv_key, conv_value, decay_log, beta_gate, init_state, live_rows, grad_out, state_grad_in):

    def forward(p_query, p_key, p_value, c_query, c_key, c_value, d_log, b_gate, s_init):
        return core(p_query, p_key, p_value, c_query, c_key, c_value, d_log, b_gate, s_init, live_rows)
    primal, pullback = jax.vjp(forward, proj_query, proj_key, proj_value, conv_query, conv_key, conv_value, decay_log, beta_gate, init_state)
    return pullback((grad_out.astype(jnp.float32), state_grad_in))

def reference(hidden, w_query, w_key, w_value, conv_query, conv_key, conv_value, decay_log, beta_gate, init_state, grad_out, state_grad_in, rollout_lengths, slot_map):
    proj_query = jnp.dot(hidden.astype(jnp.float32), w_query.astype(jnp.float32), preferred_element_type=jnp.float32).astype(jnp.bfloat16)
    proj_key = jnp.dot(hidden.astype(jnp.float32), w_key.astype(jnp.float32), preferred_element_type=jnp.float32).astype(jnp.bfloat16)
    proj_value = jnp.dot(hidden.astype(jnp.float32), w_value.astype(jnp.float32), preferred_element_type=jnp.float32).astype(jnp.bfloat16)
    position = jnp.arange(WINDOW_LENGTH, dtype=jnp.int32)
    live_rows = (position[None, :] < rollout_lengths[:, None]).astype(jnp.float32).reshape(TOTAL_ROWS)

    def per_device(array_in):
        return array_in.reshape((N_BATCH, array_in.shape[0] // N_BATCH) + array_in.shape[1:])

    def one_block(pieces):
        return core_grads(pieces[0], pieces[1], pieces[2], conv_query, conv_key, conv_value, pieces[3], pieces[4], pieces[5], pieces[6], pieces[7], pieces[8])
    results = lax.map(one_block, (per_device(proj_query), per_device(proj_key), per_device(proj_value), per_device(decay_log), per_device(beta_gate), per_device(init_state), per_device(live_rows), per_device(grad_out), per_device(state_grad_in)))
    d_query = results[0].reshape(TOTAL_ROWS, -1)
    d_key = results[1].reshape(TOTAL_ROWS, -1)
    d_value = results[2].reshape(TOTAL_ROWS, -1)
    grad_conv_query = lax.optimization_barrier(jnp.sum(results[3], axis=0))
    grad_conv_key = lax.optimization_barrier(jnp.sum(results[4], axis=0))
    grad_conv_value = lax.optimization_barrier(jnp.sum(results[5], axis=0))
    grad_decay = results[6].reshape(TOTAL_ROWS, VALUE_HEADS)
    grad_beta = results[7].reshape(TOTAL_ROWS, VALUE_HEADS)
    grad_init = results[8].reshape(REQS, VALUE_HEADS, DK, DV)

    def shard_cols(array_in):
        return jnp.moveaxis(array_in.reshape(array_in.shape[0], N_TENSOR, -1), 1, 0)

    def add_shard(running, pieces):
        contract = (((1,), (1,)), ((), ()))
        shard_term = lax.dot_general(pieces[0].astype(jnp.float32), pieces[1].astype(jnp.float32), contract, preferred_element_type=jnp.float32)
        shard_term = shard_term + lax.dot_general(pieces[2].astype(jnp.float32), pieces[3].astype(jnp.float32), contract, preferred_element_type=jnp.float32)
        shard_term = shard_term + lax.dot_general(pieces[4].astype(jnp.float32), pieces[5].astype(jnp.float32), contract, preferred_element_type=jnp.float32)
        rounded = lax.optimization_barrier(shard_term.astype(jnp.bfloat16))
        return (running + rounded.astype(jnp.float32), None)
    stacked = (shard_cols(d_query), shard_cols(w_query), shard_cols(d_key), shard_cols(w_key), shard_cols(d_value), shard_cols(w_value))
    summed, unused = lax.scan(add_shard, jnp.zeros((TOTAL_ROWS, D), jnp.float32), stacked)
    grad_hidden = summed.astype(jnp.bfloat16)
    transposed = hidden.T
    grad_w_query = jnp.dot(transposed.astype(jnp.float32), d_query.astype(jnp.float32), preferred_element_type=jnp.float32)
    grad_w_key = jnp.dot(transposed.astype(jnp.float32), d_key.astype(jnp.float32), preferred_element_type=jnp.float32)
    grad_w_value = jnp.dot(transposed.astype(jnp.float32), d_value.astype(jnp.float32), preferred_element_type=jnp.float32)
    slot_state_grad = jnp.zeros_like(grad_init).at[slot_map].set(grad_init)
    return (grad_hidden, grad_w_query, grad_w_key, grad_w_value, grad_conv_query, grad_conv_key, grad_conv_value, grad_decay, grad_beta, slot_state_grad)
```

```python
import functools
import jax
import jax.numpy as jnp
from jax import lax
from jax.experimental import pallas as pl
from jax.experimental.pallas import tpu as pltpu
from jax.sharding import PartitionSpec as P

EPSILON = 1e-06
F32 = jnp.float32
BF16 = jnp.bfloat16
NN = (((1,), (0,)), ((), ()))
NT = (((1,), (1,)), ((), ()))
TN = (((0,), (0,)), ((), ()))


def dot(a, b, dims=NN):
    return lax.dot_general(a.astype(BF16), b.astype(BF16), dims, preferred_element_type=F32)


def exact_dot(a, b, dims=NN):
    return lax.dot_general(
        a, b, dims, preferred_element_type=F32, precision=lax.Precision.HIGHEST
    )


def shift_down(x, count, rows):
    if count == 0:
        return x
    return jnp.where(rows >= count, pltpu.roll(x, count, 0), 0.0)


def shift_up(x, count, rows):
    if count == 0:
        return x
    size = x.shape[0]
    return jnp.where(rows < size - count, pltpu.roll(x, size - count, 0), 0.0)


def unit_lower_inverse(couplings, rows, cols):
    size = rows.shape[0]
    one = (rows == cols).astype(F32)
    first = (rows % 2 == 1) & (cols == rows - 1)
    inverses = [one - jnp.where(first, a, 0.0) for a in couplings]
    block = 2
    while block < min(8, size):
        mask = ((rows // block) % 2 == 1) & (cols // block == rows // block - 1)
        inner = [dot(t, jnp.where(mask, a, 0.0)) for t, a in zip(inverses, couplings)]
        inverses = [t - dot(x, t) for t, x in zip(inverses, inner)]
        block *= 2
    while block < size:
        count = size // (2 * block)
        half_rows = lax.broadcasted_iota(jnp.int32, (size // 2, size), 0)
        half_cols = lax.broadcasted_iota(jnp.int32, (size // 2, size), 1)
        mask = half_cols // block == 2 * (half_rows // block)
        odd = [
            jnp.concatenate(
                [t[(2 * i + 1) * block : (2 * i + 2) * block] for i in range(count)], axis=0
            )
            for t in inverses
        ]
        inner = [jnp.where(mask, dot(o, a), 0.0) for o, a in zip(odd, couplings)]
        odd = [o - dot(x, t) for o, x, t in zip(odd, inner, inverses)]
        inverses = [
            jnp.concatenate(
                [
                    piece
                    for i in range(count)
                    for piece in (
                        t[2 * i * block : (2 * i + 1) * block],
                        o[i * block : (i + 1) * block],
                    )
                ],
                axis=0,
            )
            for t, o in zip(inverses, odd)
        ]
        block *= 2
    return inverses


def core_kernel(
    key_heads,
    group,
    lengths,
    places,
    proj_q,
    proj_k,
    proj_v,
    taps_q,
    taps_k,
    taps_v,
    decay,
    beta,
    init_state,
    grad_out,
    state_grad,
    grads,
    grad_taps,
    grad_decay,
    grad_beta,
    grad_init,
):
    step = pl.program_id(0)
    size = proj_q.shape[0]
    width = init_state.shape[-1]
    heads = key_heads * group
    rows = lax.broadcasted_iota(jnp.int32, (size, size), 0)
    cols = lax.broadcasted_iota(jnp.int32, (size, size), 1)
    wide_rows = lax.broadcasted_iota(jnp.int32, (size, width), 0)
    length = lengths[step]
    causal = rows >= cols
    strict = rows > cols
    lower = causal.astype(F32)
    upper = (rows <= cols).astype(F32)
    one = (rows == cols).astype(F32)
    live_row = (lax.broadcasted_iota(jnp.int32, (heads, size), 1) < length).astype(F32)
    live_col = (lax.broadcasted_iota(jnp.int32, (size, heads), 0) < length).astype(F32)
    live_wide = (wide_rows < length).astype(F32)

    gate_row = decay[0] * live_row
    rate_row = beta[0] * live_row
    cum_row = exact_dot(gate_row, lower, NT)
    cum_col = exact_dot(lower, gate_row, NT)
    rate_col = exact_dot(one, rate_row, NT)
    last_row = cum_row[:, size - 1 :]
    growth_col = jnp.exp(cum_col)

    def prepare(ref, taps, index):
        cut = slice(index * width, (index + 1) * width)
        x = ref[:, cut].astype(F32)
        mixed = x * taps[3:4, cut]
        for i in range(3):
            mixed = mixed + shift_down(x, 3 - i, wide_rows) * taps[i : i + 1, cut]
        gate = 1.0 / (1.0 + jnp.exp(-mixed))
        active = mixed * gate
        return active, gate + active * (1.0 - gate)

    def unit(active, factor):
        total = jnp.sum(active * active, axis=-1, keepdims=True) + EPSILON
        scale = factor * lax.rsqrt(total)
        return active * scale, scale, 1.0 / total

    q_in = [prepare(proj_q, taps_q, i) for i in range(key_heads)]
    k_in = [prepare(proj_k, taps_k, i) for i in range(key_heads)]
    v_in = [prepare(proj_v, taps_v, i) for i in range(heads)]
    q_unit = [unit(x[0], width ** (-0.5)) for x in q_in]
    k_unit = [unit(x[0], 1.0) for x in k_in]
    q_f = [x[0] for x in q_unit]
    k_f = [x[0] for x in k_unit]
    q_b = [x.astype(BF16) for x in q_f]
    k_b = [x.astype(BF16) for x in k_f]
    kk = [dot(k, k, NT) for k in k_b]
    qk = [dot(q, k, NT) for q, k in zip(q_b, k_b)]
    kq = [dot(k, q, NT) for q, k in zip(q_b, k_b)]

    cum_c = [cum_col[:, h : h + 1] for h in range(heads)]
    cum_r = [cum_row[h : h + 1, :] for h in range(heads)]
    rate = [rate_col[:, h : h + 1] for h in range(heads)]
    growth = [growth_col[:, h : h + 1] for h in range(heads)]
    final = [jnp.exp(last_row[h : h + 1, :]) for h in range(heads)]
    rest = [jnp.exp(last_row[h : h + 1, :] - cum_c[h]) for h in range(heads)]
    within = [
        jnp.where(causal, jnp.exp(jnp.where(causal, cum_c[h] - cum_r[h], 0.0)), 0.0)
        for h in range(heads)
    ]
    within_t = [
        jnp.where(rows <= cols, jnp.exp(jnp.where(rows <= cols, cum_r[h] - cum_c[h], 0.0)), 0.0)
        for h in range(heads)
    ]
    couplings = [
        jnp.where(strict, rate[h] * kk[h // group] * within[h], 0.0) for h in range(heads)
    ]
    inverses = [t.astype(BF16) for t in unit_lower_inverse(couplings, rows, cols)]

    s_f = [init_state[0, h] for h in range(heads)]
    ds_f = [state_grad[0, h] for h in range(heads)]
    s_b = [x.astype(BF16) for x in s_f]
    ds_b = [x.astype(BF16) for x in ds_f]
    k_s = [dot(k_b[h // group], s_b[h]) for h in range(heads)]
    left = [v_in[h][0] - growth[h] * k_s[h] for h in range(heads)]
    new_b = [dot(inverses[h], rate[h] * left[h]).astype(BF16) for h in range(heads)]
    out_b = [
        (grad_out[:, h * width : (h + 1) * width].astype(F32) * live_wide).astype(BF16)
        for h in range(heads)
    ]
    d_new = [
        dot(kq[h // group] * within_t[h], out_b[h]) + rest[h] * dot(k_b[h // group], ds_b[h])
        for h in range(heads)
    ]
    d_right = [dot(inverses[h], d_new[h], TN) for h in range(heads)]
    d_scores = [dot(out_b[h], new_b[h], NT) * within[h] for h in range(heads)]
    d_coup = [
        jnp.where(strict, -dot(d_right[h], new_b[h], NT) * within[h], 0.0) for h in range(heads)
    ]
    back_b = [(-(rate[h] * growth[h]) * d_right[h]).astype(BF16) for h in range(heads)]
    u_q = [growth[h] * dot(out_b[h], s_b[h], NT) for h in range(heads)]
    u_k = [dot(back_b[h], s_b[h], NT) for h in range(heads)]
    u_e = [rest[h] * dot(new_b[h], ds_b[h], NT) for h in range(heads)]
    cum_from_rows = []
    cum_from_cols = []
    rate_grads = []
    last_grads = []
    for h in range(heads):
        g = h // group
        y = d_coup[h] * kk[g]
        y_row = jnp.sum(y, axis=-1, keepdims=True)
        scored = d_scores[h] * qk[g]
        ended = jnp.sum(k_f[g] * u_e[h], axis=-1, keepdims=True)
        rate_grads.append(jnp.sum(d_right[h] * left[h], axis=-1, keepdims=True) + y_row)
        direct = q_f[g] * u_q[h] + k_f[g] * u_k[h] + scored
        cum_from_rows.append(
            jnp.sum(direct, axis=-1, keepdims=True) + rate[h] * y_row - ended
        )
        cum_from_cols.append(jnp.sum(scored + rate[h] * y, axis=0, keepdims=True))
        last_grads.append(
            jnp.sum(ended, axis=0, keepdims=True)
            + final[h] * jnp.sum(jnp.sum(ds_f[h] * s_f[h], axis=-1, keepdims=True), axis=0, keepdims=True)
        )
        grad_init[0, h] = (
            final[h] * ds_f[h]
            + dot(q_b[g], growth[h] * out_b[h].astype(F32), TN)
            + dot(k_b[g], back_b[h], TN)
        ).astype(BF16)
    gate_grad = exact_dot(upper, jnp.concatenate(cum_from_rows, axis=1))
    gate_grad = gate_grad - exact_dot(upper, jnp.concatenate(cum_from_cols, axis=0), NT)
    gate_grad = gate_grad + jnp.concatenate(last_grads, axis=1)
    grad_decay[...] = gate_grad * live_col
    grad_beta[...] = jnp.concatenate(rate_grads, axis=1) * live_col

    @pl.when(step == 0)
    def _():
        grad_taps[...] = jnp.zeros_like(grad_taps)

    def conv_back(d_active, slope, ref, taps, index, offset):
        cut = slice(index * width, (index + 1) * width)
        place = slice(offset + index * width, offset + (index + 1) * width)
        x = ref[:, cut].astype(F32)
        d_mixed = d_active * slope
        d_x = d_mixed * taps[3:4, cut]
        sums = []
        for i in range(3):
            d_x = d_x + shift_up(d_mixed, 3 - i, wide_rows) * taps[i : i + 1, cut]
            sums.append(jnp.sum(d_mixed * shift_down(x, 3 - i, wide_rows), axis=0, keepdims=True))
        sums.append(jnp.sum(d_mixed * x, axis=0, keepdims=True))
        grads[:, place] = d_x.astype(BF16)
        grad_taps[:, place] += jnp.concatenate(sums, axis=0)

    def unit_back(d_unit, unit_in):
        unit_rows, scale, inverse_total, active = unit_in
        inner = jnp.sum(d_unit * active, axis=-1, keepdims=True)
        return scale * (d_unit - active * (inner * inverse_total))

    for g in range(key_heads):
        members = range(g * group, (g + 1) * group)
        scores_sum = sum(d_scores[h] for h in members).astype(BF16)
        kk_sum = sum(rate[h] * d_coup[h] for h in members).astype(BF16)
        d_q = sum(u_q[h] for h in members) + dot(scores_sum, k_b[g])
        d_k = sum(u_k[h] + u_e[h] for h in members)
        d_k = d_k + dot(scores_sum, q_b[g], TN) + dot(kk_sum, k_b[g]) + dot(kk_sum, k_b[g], TN)
        d_q = unit_back(d_q, q_unit[g] + (q_in[g][0],))
        d_k = unit_back(d_k, k_unit[g] + (k_in[g][0],))
        conv_back(d_q, q_in[g][1], proj_q, taps_q, g, 0)
        conv_back(d_k, k_in[g][1], proj_k, taps_k, g, key_heads * width)
    for h in range(heads):
        conv_back(rate[h] * d_right[h], v_in[h][1], proj_v, taps_v, h, 2 * key_heads * width)


def core_call(proj_q, proj_k, proj_v, taps_q, taps_k, taps_v, decay, beta, init_state, grad_out, state_grad, lengths, places, out_places):
    requests, heads, width, _ = init_state.shape
    size = proj_q.shape[0] // requests
    key_heads = proj_q.shape[1] // width
    columns = proj_q.shape[1] * 2 + proj_v.shape[1]

    def rows_of(array):
        return pl.BlockSpec((size, array.shape[1]), lambda r, *_: (r, 0))

    def fixed(array):
        return pl.BlockSpec(array.shape, lambda r, *_: (0,) * array.ndim)

    by_request = pl.BlockSpec((1, heads, size), lambda r, *_: (r, 0, 0))
    state = pl.BlockSpec((1, heads, width, width), lambda r, *_: (r, 0, 0, 0))
    return pl.pallas_call(
        functools.partial(core_kernel, key_heads, heads // key_heads),
        grid_spec=pltpu.PrefetchScalarGridSpec(
            num_scalar_prefetch=2,
            grid=(requests,),
            in_specs=[
                rows_of(proj_q), rows_of(proj_k), rows_of(proj_v),
                fixed(taps_q), fixed(taps_k), fixed(taps_v),
                by_request, by_request, state, rows_of(grad_out), state,
            ],
            out_specs=[
                pl.BlockSpec((size, columns), lambda r, *_: (r, 0)),
                pl.BlockSpec((taps_q.shape[0], columns), lambda r, *_: (0, 0)),
                pl.BlockSpec((size, heads), lambda r, *_: (r, 0)),
                pl.BlockSpec((size, heads), lambda r, *_: (r, 0)),
                pl.BlockSpec((1, heads, width, width), lambda r, lengths, places: (places[r], 0, 0, 0)),
            ],
        ),
        out_shape=[
            jax.ShapeDtypeStruct((requests * size, columns), BF16),
            jax.ShapeDtypeStruct((taps_q.shape[0], columns), F32),
            jax.ShapeDtypeStruct((requests * size, heads), F32),
            jax.ShapeDtypeStruct((requests * size, heads), F32),
            jax.ShapeDtypeStruct((out_places, heads, width, width), BF16),
        ],
        compiler_params=pltpu.CompilerParams(vmem_limit_bytes=48 << 20),
        name="core_grads",
    )(lengths, places, proj_q, proj_k, proj_v, taps_q, taps_k, taps_v, decay, beta, init_state, grad_out, state_grad)


def place_kernel(sources, ranks, *refs):
    received, out = refs[:-1], refs[-1]
    step = pl.program_id(0)
    for index, block in enumerate(received):

        @pl.when(sources[step] == index)
        def _():
            out[...] = block[...].astype(out.dtype)


def place_states(sources, ranks, received):
    requests = sources.shape[0]
    block = (1,) + received[0].shape[1:]

    def pick(index):
        def index_map(r, sources, ranks):
            return (jnp.where(sources[r] == index, ranks[r], 0), 0, 0, 0)

        return index_map

    return pl.pallas_call(
        place_kernel,
        grid_spec=pltpu.PrefetchScalarGridSpec(
            num_scalar_prefetch=2,
            grid=(requests,),
            in_specs=[pl.BlockSpec(block, pick(i)) for i in range(len(received))],
            out_specs=pl.BlockSpec(block, lambda r, *_: (r, 0, 0, 0)),
        ),
        out_shape=jax.ShapeDtypeStruct((requests,) + block[1:], F32),
        compiler_params=pltpu.CompilerParams(vmem_limit_bytes=32 << 20),
        name="place_states",
    )(sources, ranks, *received)


def slot_plan(slot_map, all_slots, me, parts):
    requests = slot_map.shape[0]
    capacity = max(1, requests // parts)
    owners = all_slots // requests
    request_ids = jnp.arange(all_slots.shape[0], dtype=jnp.int32)
    earlier = (
        (request_ids[:, None] > request_ids[None, :])
        & (request_ids[:, None] // requests == request_ids[None, :] // requests)
        & (owners[:, None] == owners[None, :])
    )
    ranks = jnp.sum(earlier.astype(jnp.int32), axis=1)
    hops = jnp.bitwise_xor(owners, request_ids // requests)
    places = lax.dynamic_slice_in_dim(hops * capacity + ranks, me * requests, requests)
    own_slots = me * requests + jnp.arange(requests, dtype=jnp.int32)
    matches = (all_slots[None, :] == own_slots[:, None]).astype(jnp.int32)
    sources = jnp.sum(matches * hops[None, :], axis=1)
    source_ranks = jnp.sum(matches * ranks[None, :], axis=1)
    return places, sources, source_ranks, capacity


def swap(array, axis, parts, hop):
    return lax.ppermute(array, axis, [(i, i ^ hop) for i in range(parts)])


def body(
    hidden, w_query, w_key, w_value, conv_query, conv_key, conv_value, decay_log, beta_gate,
    init_state, grad_out, state_grad_in, rollout_lengths, slot_map,
):
    parts = lax.axis_size("batch")
    me = lax.axis_index("batch")
    requests = rollout_lengths.shape[0]
    size = hidden.shape[0] // requests
    heads = init_state.shape[1]
    all_slots = lax.all_gather(slot_map, "batch", axis=0, tiled=True)
    features = lax.all_gather(hidden, "tensor", axis=1, tiled=True)
    places, sources, ranks, capacity = slot_plan(slot_map, all_slots, me, parts)
    proj = [
        jnp.dot(features, w, preferred_element_type=F32).astype(BF16)
        for w in (w_query, w_key, w_value)
    ]

    def by_head(array):
        return array.reshape(requests, size, heads).transpose(0, 2, 1)

    grads, grad_taps, grad_decay, grad_beta, sent = core_call(
        *proj, conv_query, conv_key, conv_value, by_head(decay_log), by_head(beta_gate),
        init_state, grad_out, state_grad_in, rollout_lengths, places, parts * capacity,
    )
    partial = lax.dot_general(features, grads, TN, preferred_element_type=F32).astype(BF16)
    blocks = partial.reshape(parts, -1, partial.shape[1])
    received = [
        swap(lax.dynamic_index_in_dim(blocks, me ^ hop, 0, False), "batch", parts, hop)
        for hop in range(1, parts)
    ]
    weight_grads = lax.dynamic_index_in_dim(blocks, me, 0, False).astype(F32)
    for block in received:
        weight_grads = weight_grads + block.astype(F32)
    q_cols, k_cols = w_query.shape[1], w_key.shape[1]
    grad_w = (
        weight_grads[:, :q_cols],
        weight_grads[:, q_cols : q_cols + k_cols],
        weight_grads[:, q_cols + k_cols :],
    )
    weights = jnp.concatenate([w_query, w_key, w_value], axis=1)
    term = lax.dot_general(weights, grads, NT, preferred_element_type=F32).astype(BF16)
    grad_hidden = lax.psum_scatter(term, "tensor", scatter_dimension=0, tiled=True).T
    hop = 1
    while hop < parts:
        grad_taps = grad_taps + swap(grad_taps, "batch", parts, hop)
        hop *= 2
    states = [sent[i * capacity : (i + 1) * capacity] for i in range(parts)]
    states = [states[0]] + [swap(states[i], "batch", parts, i) for i in range(1, parts)]
    slot_state_grad = place_states(sources, ranks, states)
    return (
        grad_hidden, *grad_w, grad_taps[:, :q_cols], grad_taps[:, q_cols : q_cols + k_cols],
        grad_taps[:, q_cols + k_cols :], grad_decay, grad_beta, slot_state_grad,
    )


def solution(mesh):
    placed = (
        P("batch", "tensor"),
        P(None, "tensor"),
        P(None, "tensor"),
        P(None, "tensor"),
        P(None, "tensor"),
        P(None, "tensor"),
        P(None, "tensor"),
        P("batch", "tensor"),
        P("batch", "tensor"),
        P("batch", "tensor", None, None),
        P("batch", "tensor"),
        P("batch", "tensor", None, None),
        P("batch"),
        P("batch"),
    )
    return jax.shard_map(
        body,
        mesh=mesh,
        in_specs=placed,
        out_specs=(
            P("batch", "tensor"),
            P("batch", "tensor"),
            P("batch", "tensor"),
            P("batch", "tensor"),
            P(None, "tensor"),
            P(None, "tensor"),
            P(None, "tensor"),
            P("batch", "tensor"),
            P("batch", "tensor"),
            P("batch", "tensor", None, None),
        ),
        check_vma=False,
    )
```

```python
import functools
import jax
import jax.numpy as jnp
from jax import lax
from jax.experimental import pallas as pl
from jax.experimental.pallas import tpu as pltpu
from jax.sharding import PartitionSpec as P

EPSILON = 1e-06
F32 = jnp.float32
BF16 = jnp.bfloat16
NN = (((1,), (0,)), ((), ()))
NT = (((1,), (1,)), ((), ()))
TN = (((0,), (0,)), ((), ()))


def dot(a, b, dims=NN):
    return lax.dot_general(a.astype(BF16), b.astype(BF16), dims, preferred_element_type=F32)


def exact_dot(a, b, dims=NN):
    return lax.dot_general(
        a, b, dims, preferred_element_type=F32, precision=lax.Precision.HIGHEST
    )


def shift_down(x, count, rows):
    return jnp.where(rows >= count, pltpu.roll(x, count, 0), 0.0)


def shift_up(x, count, rows):
    size = x.shape[0]
    return jnp.where(rows < size - count, pltpu.roll(x, size - count, 0), 0.0)


def unit_lower_inverse(couplings, rows, cols):
    size = rows.shape[0]
    one = (rows == cols).astype(F32)
    first = (rows % 2 == 1) & (cols == rows - 1)
    inverses = [one - jnp.where(first, a, 0.0) for a in couplings]
    couplings = [a.astype(BF16) for a in couplings]
    block = 2
    while block < min(8, size):
        mask = ((rows // block) % 2 == 1) & (cols // block == rows // block - 1)
        inner = [dot(t, a) for t, a in zip(inverses, couplings)]
        inner = [jnp.where(mask, x, 0.0) for x in inner]
        inverses = [t - dot(x, t) for t, x in zip(inverses, inner)]
        block *= 2
    while block < size:
        count = size // (2 * block)
        half_rows = lax.broadcasted_iota(jnp.int32, (size // 2, size), 0)
        half_cols = lax.broadcasted_iota(jnp.int32, (size // 2, size), 1)
        mask = half_cols // block == 2 * (half_rows // block)
        odd = [
            jnp.concatenate(
                [t[(2 * i + 1) * block : (2 * i + 2) * block] for i in range(count)], axis=0
            )
            for t in inverses
        ]
        inner = [jnp.where(mask, dot(o, a), 0.0) for o, a in zip(odd, couplings)]
        odd = [o - dot(x, t) for o, x, t in zip(odd, inner, inverses)]
        inverses = [
            jnp.concatenate(
                [
                    piece
                    for i in range(count)
                    for piece in (
                        t[2 * i * block : (2 * i + 1) * block],
                        o[i * block : (i + 1) * block],
                    )
                ],
                axis=0,
            )
            for t, o in zip(inverses, odd)
        ]
        block *= 2
    return inverses


def core_kernel(first_request, first_head, together, key_heads, later, *refs):
    lengths, places = refs[:2]
    proj, taps, (decay, beta, init_state, grad_out, state_grad) = refs[2:5], refs[5:8], refs[8:13]
    refs = refs[13:]
    if later:
        old_taps, refs = refs[:3], refs[4:]
    grads, grad_taps = refs[:3], refs[3:6]
    grad_decay, grad_beta, sent, held, sem = refs[6:]
    step = pl.program_id(0)
    width = init_state.shape[-1]
    size = proj[0].shape[0] // together
    heads = init_state.shape[1]
    group = heads // key_heads
    rows = lax.broadcasted_iota(jnp.int32, (size, size), 0)
    cols = lax.broadcasted_iota(jnp.int32, (size, size), 1)
    wide_rows = lax.broadcasted_iota(jnp.int32, (size, width), 0)
    causal = rows >= cols
    strict = rows > cols
    lower = causal.astype(F32)
    upper = (rows <= cols).astype(F32)
    one = (rows == cols).astype(F32)

    units = [(r, g) for r in range(together) for g in range(key_heads)]
    pairs = [(r, h) for r in range(together) for h in range(heads)]
    unit_of = {(r, h): r * key_heads + h // group for r, h in pairs}
    spans = [slice(r * size, (r + 1) * size) for r in range(together)]
    request = [first_request + step * together + r for r in range(together)]
    length = [lengths[x] for x in request]
    live_row = [
        (lax.broadcasted_iota(jnp.int32, (heads, size), 1) < n).astype(F32) for n in length
    ]
    live_col = [
        (lax.broadcasted_iota(jnp.int32, (size, heads), 0) < n).astype(F32) for n in length
    ]
    live_wide = [(wide_rows < n).astype(F32) for n in length]
    picked = slice(first_head, first_head + heads)
    gate_row = [decay[r, picked, :] * live_row[r] for r in range(together)]
    rate_row = [beta[r, picked, :] * live_row[r] for r in range(together)]
    cum_row = [exact_dot(x, lower, NT) for x in gate_row]
    cum_col = [exact_dot(lower, x, NT) for x in gate_row]
    rate_col = [exact_dot(one, x, NT) for x in rate_row]
    growth_col = [jnp.exp(x) for x in cum_col]

    def prepare(r, kind, index):
        cut = slice(index * width, (index + 1) * width)
        x = proj[kind][spans[r], cut].astype(F32)
        mixed = x * taps[kind][3:4, cut]
        for i in range(3):
            mixed = mixed + shift_down(x, 3 - i, wide_rows) * taps[kind][i : i + 1, cut]
        gate = 1.0 / (1.0 + jnp.exp(-mixed))
        active = mixed * gate
        return active, gate + active * (1.0 - gate)

    def unit(active, factor):
        total = jnp.sum(active * active, axis=-1, keepdims=True) + EPSILON
        scale = factor * lax.rsqrt(total)
        return active * scale, scale, 1.0 / total

    q_in = [prepare(r, 0, g) for r, g in units]
    k_in = [prepare(r, 1, g) for r, g in units]
    v_in = [prepare(r, 2, h) for r, h in pairs]
    q_unit = [unit(x[0], width ** (-0.5)) for x in q_in]
    k_unit = [unit(x[0], 1.0) for x in k_in]
    q_f = [x[0] for x in q_unit]
    k_f = [x[0] for x in k_unit]
    q_b = [x.astype(BF16) for x in q_f]
    k_b = [x.astype(BF16) for x in k_f]
    kk = [dot(k, k, NT) for k in k_b]
    qk = [dot(q, k, NT) for q, k in zip(q_b, k_b)]
    kq = [dot(k, q, NT) for q, k in zip(q_b, k_b)]

    every = range(len(pairs))
    of = [unit_of[p] for p in pairs]
    cum_c = [cum_col[r][:, h : h + 1] for r, h in pairs]
    cum_r = [cum_row[r][h : h + 1, :] for r, h in pairs]
    rate = [rate_col[r][:, h : h + 1] for r, h in pairs]
    growth = [growth_col[r][:, h : h + 1] for r, h in pairs]
    last = [x[:, size - 1 :] for x in cum_r]
    final = [jnp.exp(x) for x in last]
    rest = [jnp.exp(last[i] - cum_c[i]) for i in every]
    within = [jnp.exp(jnp.where(causal, cum_c[i] - cum_r[i], -jnp.inf)) for i in every]
    within_t = [jnp.exp(jnp.where(rows <= cols, cum_r[i] - cum_c[i], -jnp.inf)) for i in every]
    couplings = [jnp.where(strict, rate[i] * kk[of[i]] * within[i], 0.0) for i in every]
    inverses = [t.astype(BF16) for t in unit_lower_inverse(couplings, rows, cols)]

    s_b = [init_state[r, h].astype(BF16) for r, h in pairs]
    ds_b = [state_grad[r, h].astype(BF16) for r, h in pairs]
    k_s = [dot(k_b[of[i]], s_b[i]) for i in every]
    left = [v_in[i][0] - growth[i] * k_s[i] for i in every]
    new_b = [dot(inverses[i], rate[i] * left[i]).astype(BF16) for i in every]
    out_b = [
        (grad_out[spans[r], h * width : (h + 1) * width].astype(F32) * live_wide[r]).astype(BF16)
        for r, h in pairs
    ]
    d_new = [
        dot(kq[of[i]] * within_t[i], out_b[i]) + rest[i] * dot(k_b[of[i]], ds_b[i]) for i in every
    ]
    d_right = [dot(inverses[i], d_new[i], TN) for i in every]
    d_scores = [dot(out_b[i], new_b[i], NT) * within[i] for i in every]
    d_coup = [
        jnp.where(strict, -dot(d_right[i], new_b[i], NT) * within[i], 0.0) for i in every
    ]
    back_b = [(-(rate[i] * growth[i]) * d_right[i]).astype(BF16) for i in every]
    u_q = [growth[i] * dot(out_b[i], s_b[i], NT) for i in every]
    u_k = [dot(back_b[i], s_b[i], NT) for i in every]
    u_e = [rest[i] * dot(new_b[i], ds_b[i], NT) for i in every]

    def leave(r):
        return pltpu.make_async_copy(
            held.at[r],
            sent.at[places[first_request + step * together + r], pl.ds(first_head, heads)],
            sem.at[r],
        )

    @pl.when(step > 0)
    def _():
        for r in range(together):
            leave(r).wait()

    cum_from_rows, cum_from_cols, rate_grads, last_grads = [], [], [], []
    for i, (r, h) in enumerate(pairs):
        u = of[i]
        y = d_coup[i] * kk[u]
        y_row = jnp.sum(y, axis=-1, keepdims=True)
        scored = d_scores[i] * qk[u]
        ended = jnp.sum(k_f[u] * u_e[i], axis=-1, keepdims=True)
        rate_grads.append(jnp.sum(d_right[i] * left[i], axis=-1, keepdims=True) + y_row)
        direct = q_f[u] * u_q[i] + k_f[u] * u_k[i] + scored
        cum_from_rows.append(jnp.sum(direct, axis=-1, keepdims=True) + rate[i] * y_row - ended)
        cum_from_cols.append(jnp.sum(scored + rate[i] * y, axis=0, keepdims=True))
        carried = jnp.sum(state_grad[r, h] * init_state[r, h], axis=0, keepdims=True)
        last_grads.append(
            jnp.sum(ended, axis=0, keepdims=True)
            + final[i] * jnp.sum(carried, axis=1, keepdims=True)
        )
        held[r, h] = (
            final[i] * state_grad[r, h]
            + dot(q_b[u], growth[i] * out_b[i].astype(F32), TN)
            + dot(k_b[u], back_b[i], TN)
        ).astype(BF16)
    for r in range(together):
        leave(r).start()
    for r in range(together):
        mine = [i for i in every if pairs[i][0] == r]
        gate_grad = exact_dot(upper, jnp.concatenate([cum_from_rows[i] for i in mine], axis=1))
        gate_grad = gate_grad - exact_dot(
            upper, jnp.concatenate([cum_from_cols[i] for i in mine], axis=0), NT
        )
        gate_grad = gate_grad + jnp.concatenate([last_grads[i] for i in mine], axis=1)
        grad_decay[spans[r], :] = gate_grad * live_col[r]
        grad_beta[spans[r], :] = (
            jnp.concatenate([rate_grads[i] for i in mine], axis=1) * live_col[r]
        )

    @pl.when(step == 0)
    def _():
        for i, grad_tap in enumerate(grad_taps):
            grad_tap[...] = old_taps[i][...] if later else jnp.zeros_like(grad_tap)

    def conv_back(d_active, slope, r, kind, index):
        cut = slice(index * width, (index + 1) * width)
        x = proj[kind][spans[r], cut].astype(F32)
        d_mixed = d_active * slope
        d_x = d_mixed * taps[kind][3:4, cut]
        sums = []
        for i in range(3):
            moved = shift_up(d_mixed, 3 - i, wide_rows)
            d_x = d_x + moved * taps[kind][i : i + 1, cut]
            sums.append(jnp.sum(moved * x, axis=0, keepdims=True))
        sums.append(jnp.sum(d_mixed * x, axis=0, keepdims=True))
        grads[kind][spans[r], cut] = d_x.astype(BF16)
        grad_taps[kind][:, cut] += jnp.concatenate(sums, axis=0)

    def unit_back(d_unit, unit_in, active):
        unit_rows, scale, inverse_total = unit_in
        inner = jnp.sum(d_unit * active, axis=-1, keepdims=True)
        return scale * (d_unit - active * (inner * inverse_total))

    for u, (r, g) in enumerate(units):
        members = [i for i in every if of[i] == u]
        scores_sum = sum(d_scores[i] for i in members).astype(BF16)
        kk_sum = sum(rate[i] * d_coup[i] for i in members)
        kk_sum = (kk_sum + kk_sum.T).astype(BF16)
        d_q = sum(u_q[i] for i in members) + dot(scores_sum, k_b[u])
        d_k = sum(u_k[i] + u_e[i] for i in members)
        d_k = d_k + dot(scores_sum, q_b[u], TN) + dot(kk_sum, k_b[u])
        conv_back(unit_back(d_q, q_unit[u], q_in[u][0]), q_in[u][1], r, 0, g)
        conv_back(unit_back(d_k, k_unit[u], k_in[u][0]), k_in[u][1], r, 1, g)
    for i, (r, h) in enumerate(pairs):
        conv_back(rate[i] * d_right[i], v_in[i][1], r, 2, h)

    @pl.when(step == pl.num_programs(0) - 1)
    def _():
        for r in range(together):
            leave(r).wait()


def core_call(
    together, first, count, members, proj, taps, decay, beta, init_state, grad_out, state_grad,
    lengths, places, sent_shape, before,
):
    all_heads, width = init_state.shape[1:3]
    size = decay.shape[2]
    key_heads = len(members)
    heads = key_heads * (all_heads * width // proj[0].shape[1])
    part = members[0] // key_heads
    first_head = part * heads
    widths = [key_heads * width, key_heads * width, heads * width]
    rows = count * size
    start = first // together

    def here(offset, column, columns):
        return pl.BlockSpec((together * size, columns), lambda i, *_: (offset + i, column))

    def fixed(array, column, columns):
        return pl.BlockSpec((array.shape[0], columns), lambda i, *_: (0, column))

    by_request = pl.BlockSpec((together, all_heads, size), lambda i, *_: (start + i, 0, 0))
    state = pl.BlockSpec((together, heads, width, width), lambda i, *_: (start + i, part, 0, 0))
    small = pl.BlockSpec((together * size, heads), lambda i, *_: (i, 0))
    anywhere = pl.BlockSpec(memory_space=pl.ANY)
    kept = [] if before is None else [*before[3:6], before[8]]
    kept_columns = [part if x.shape[1] > n else 0 for x, n in zip(kept, widths)]
    products = count * heads * 26 * 2 * size * width * width
    return pl.pallas_call(
        functools.partial(core_kernel, first, first_head, together, key_heads, bool(kept)),
        grid_spec=pltpu.PrefetchScalarGridSpec(
            num_scalar_prefetch=2,
            grid=(count // together,),
            in_specs=[here(0, part, n) for n in widths]
            + [fixed(x, part, n) for x, n in zip(taps, widths)]
            + [by_request, by_request, state, here(start, part, heads * width), state]
            + [fixed(x, j, n) for x, j, n in zip(kept, kept_columns, widths)]
            + [anywhere] * (len(kept) > 0),
            out_specs=[here(0, 0, n) for n in widths]
            + [fixed(x, 0, n) for x, n in zip(taps, widths)]
            + [small, small, anywhere],
            scratch_shapes=[
                pltpu.VMEM((together, heads, width, width), BF16),
                pltpu.SemaphoreType.DMA((together,)),
            ],
        ),
        out_shape=[jax.ShapeDtypeStruct((rows, n), BF16) for n in widths]
        + [jax.ShapeDtypeStruct((x.shape[0], n), F32) for x, n in zip(taps, widths)]
        + [jax.ShapeDtypeStruct((rows, heads), F32)] * 2
        + [jax.ShapeDtypeStruct(sent_shape, BF16)],
        input_output_aliases={16: 8} if kept else {},
        compiler_params=pltpu.CompilerParams(vmem_limit_bytes=50 << 20),
        cost_estimate=cost(12 * products, count * heads * 400000),
        name="core_grads",
    )(
        lengths, places, *proj, *taps, decay, beta, init_state, grad_out, state_grad, *kept
    )


COST = 10**9


def whole(array):
    return pl.BlockSpec(array.shape, lambda *_: (0,) * len(array.shape))


def cost(flops, size):
    return pl.CostEstimate(flops=flops // COST, bytes_accessed=size // COST, transcendentals=0)


def assemble_kernel(indices, *refs):
    blocks, features = refs[:-1], refs[-1]
    width = blocks[0].shape[1]
    for i, block in enumerate(blocks):
        features[:, pl.ds(pl.multiple_of(indices[i] * width, width), width)] = block[...]


def assemble(indices, blocks):
    rows, width = blocks[0].shape
    tile = 128

    def tiles(count):
        return pl.BlockSpec((tile, count), lambda i, *_: (i, 0))

    return pl.pallas_call(
        assemble_kernel,
        grid_spec=pltpu.PrefetchScalarGridSpec(
            num_scalar_prefetch=1,
            grid=(rows // tile,),
            in_specs=[tiles(width)] * len(blocks),
            out_specs=tiles(width * len(blocks)),
        ),
        out_shape=jax.ShapeDtypeStruct((rows, width * len(blocks)), BF16),
        compiler_params=pltpu.CompilerParams(vmem_limit_bytes=32 << 20),
        cost_estimate=cost(1, 4 << 20),
        name="assemble",
    )(indices, *blocks)


def term_kernel(sets, *refs):
    grads, weights, (out, held) = refs[: 3 * sets], refs[3 * sets : 3 * sets + 3], refs[-2:]
    width = out.shape[2]

    @pl.when(pl.program_id(0) == 0)
    def _():
        column = 0
        for kind in range(3):
            for g in range(sets):
                grad = grads[3 * g + kind]
                held[:, column : column + grad.shape[1]] = grad[...]
                column += grad.shape[1]

    total, column = 0.0, 0
    for weight in weights:
        total = total + dot(held[:, column : column + weight.shape[1]], weight[...], NT)
        column += weight.shape[1]
    for i in range(out.shape[0]):
        out[i] = total[:, i * width : (i + 1) * width].astype(BF16)


def head_terms(parts, sets, weights):
    rows = sets[0][0].shape[0]
    depth = weights[0].shape[0]
    columns = sum(w.shape[1] for w in weights)
    width = depth // parts
    tile = max(1, 512 // width)
    grads = [x for group in sets for x in group]
    return pl.pallas_call(
        functools.partial(term_kernel, len(sets)),
        grid=(parts // tile,),
        in_specs=[whole(x) for x in grads]
        + [pl.BlockSpec((tile * width, w.shape[1]), lambda i: (i, 0)) for w in weights],
        out_specs=pl.BlockSpec((tile, rows, width), lambda i: (i, 0, 0)),
        out_shape=jax.ShapeDtypeStruct((parts, rows, width), BF16),
        scratch_shapes=[pltpu.VMEM((rows, columns), BF16)],
        compiler_params=pltpu.CompilerParams(vmem_limit_bytes=50 << 20),
        cost_estimate=cost(2 * rows * depth * columns, 7 << 20),
        name="head_terms",
    )(*grads, *weights)


def weight_kernel(chunks, attached, order, *refs):
    features, grads = refs[:chunks], refs[chunks : 4 * chunks]
    refs = refs[4 * chunks :]
    taps, states = (refs[:attached], refs[attached]) if attached else ((), None)
    outs, turned = refs[attached + (attached > 0) : -1], refs[-1]
    step = pl.program_id(0)
    columns = sum(x.shape[1] for x in grads[:3])
    starts = [sum(x.shape[0] for x in features[:i]) for i in range(chunks)]

    @pl.when(step == 0)
    def _():
        for c, start in enumerate(starts):
            row = 0
            for grad in grads[3 * c : 3 * c + 3]:
                count, width = grad.shape
                turned[row : row + width, start : start + count] = grad[...].T
                row += width

    total = sum(
        dot(turned[:, start : start + x.shape[0]], x[...]) for start, x in zip(starts, features)
    )
    for i, out in enumerate(outs):

        @pl.when(step == i)
        def _():
            out[:columns, :] = total.astype(out.dtype)
            if attached and i < len(outs) - 1:
                attach(out, columns, i + 1, len(outs), taps, states)


def state_shape(depth, heads, width):
    across = min(depth // width, heads)
    return heads // across, across


def attach(out, row, hop, parts, taps, states):
    heads, width = states.shape[1], states.shape[2]
    capacity = states.shape[0] // parts
    down, across = state_shape(out.shape[1], heads, width)
    for k in range(capacity):
        for h in range(heads):
            place = slice((h % across) * width, (h % across + 1) * width)
            start = row + (k * down + h // across) * width
            out[start : start + width, place] = states[hop * capacity + k, h]
    row = row + capacity * down * width
    tiles = out.shape[1] // width
    for index, piece in enumerate(tap_pieces(taps, width)):
        high = piece.astype(BF16)
        low = (piece - high.astype(F32)).astype(BF16)
        block = jnp.concatenate([high.astype(F32), low.astype(F32)], axis=0)
        block = jnp.concatenate([block, jnp.zeros_like(block)], axis=0).astype(BF16)
        start = row + index // tiles * 16
        place = slice(index % tiles * width, (index % tiles + 1) * width)
        out[start : start + 16, place] = block


def tap_pieces(taps, width):
    return [
        x[:, i * width : (i + 1) * width] for x in taps for i in range(x.shape[1] // width)
    ]


def weight_blocks(order, features, grads, index, widths, taps=(), states=None):
    parts = order.shape[0]
    depth = features[0].shape[1] // parts
    columns = sum(widths)

    def of_key_head(array, width):
        place = index if array.shape[1] > width else 0
        return pl.BlockSpec((array.shape[0], width), lambda i, order: (0, place))

    rows = sum(x.shape[0] for x in features)
    extra = 0
    if taps:
        heads, width = states.shape[1], states.shape[2]
        pieces = sum(x.shape[1] for x in taps) // width
        extra = states.shape[0] // parts * state_shape(depth, heads, width)[0] * width
        extra += -(-pieces // (depth // width)) * 16
    shapes = [jax.ShapeDtypeStruct((columns + extra, depth), BF16)] * (parts - 1)
    shapes.append(jax.ShapeDtypeStruct((columns, depth), F32))
    attached = [*taps, states] if taps else []
    return pl.pallas_call(
        functools.partial(weight_kernel, len(features), len(taps)),
        grid_spec=pltpu.PrefetchScalarGridSpec(
            num_scalar_prefetch=1,
            grid=(parts,),
            in_specs=[
                pl.BlockSpec((x.shape[0], depth), lambda i, order: (0, order[i]))
                for x in features
            ]
            + [of_key_head(x, n) for group in grads for x, n in zip(group, widths)]
            + [whole(x) for x in attached],
            out_specs=[whole(x) for x in shapes],
            scratch_shapes=[pltpu.VMEM((columns, rows), BF16)],
        ),
        out_shape=shapes,
        compiler_params=pltpu.CompilerParams(vmem_limit_bytes=50 << 20),
        cost_estimate=cost(2 * rows * depth * parts * columns, 8 << 20),
        name="weight_blocks",
    )(order, *features, *[x for group in grads for x in group], *attached)


def finish_kernel(terms, widths, *refs):
    key_heads = (len(refs) - 3) // terms
    outs = refs[-3:]
    for g in range(key_heads):
        pieces = refs[g * terms : (g + 1) * terms]
        total = pieces[0][...].astype(F32)
        for piece in pieces[1:]:
            total = total + piece[...].astype(F32)
        total = total.T
        start = 0
        for out, width in zip(outs, widths):
            out[:, g * width : (g + 1) * width] = total[:, start : start + width]
            start += width


def finish_weights(pieces, widths):
    key_heads, terms, rows = len(pieces), len(pieces[0]), pieces[0][0].shape[1]
    tile = min(rows, 128)
    sizes = [key_heads * n for n in widths]
    return pl.pallas_call(
        functools.partial(finish_kernel, terms, widths),
        grid=(rows // tile,),
        in_specs=[pl.BlockSpec((sum(widths), tile), lambda i: (0, i))] * (key_heads * terms),
        out_specs=[pl.BlockSpec((tile, n), lambda i: (i, 0)) for n in sizes],
        out_shape=[jax.ShapeDtypeStruct((rows, n), F32) for n in sizes],
        compiler_params=pltpu.CompilerParams(vmem_limit_bytes=32 << 20),
        cost_estimate=pl.CostEstimate(flops=10**12, bytes_accessed=10**9, transcendentals=0),
        name="finish_weights",
    )(*[x for group in pieces for x in group])


def place_kernel(shape, first_tap_row, taps_count, sources, ranks, *refs):
    taps, kept = refs[:taps_count], refs[taps_count]
    hops = (len(refs) - taps_count - 5) // 2
    received = refs[taps_count + 1 : taps_count + 1 + hops]
    edges = refs[taps_count + 1 + hops : taps_count + 1 + 2 * hops]
    out, tap_outs = refs[-4], refs[-3:]
    heads, width = out.shape[1], out.shape[2]
    down, across = shape
    step = pl.program_id(0)
    for j in range(out.shape[0]):
        source, rank = sources[step * out.shape[0] + j], ranks[step * out.shape[0] + j]

        @pl.when(source == 0)
        def _():
            out[j] = kept[rank].astype(F32)

        for index, block in enumerate(received):

            @pl.when(source == index + 1)
            def _():
                for h in range(heads):
                    start = pl.multiple_of((rank * down + h // across) * width, width)
                    place = slice(h % across * width, (h % across + 1) * width)
                    out[j, h] = block[pl.ds(start, width), place].astype(F32)

    @pl.when(step == 0)
    def _():
        tiles = edges[0].shape[1] // width
        index, columns = 0, [0, 0, 0]
        for t, mine in enumerate(taps):
            for i in range(mine.shape[1] // width):
                piece = mine[:, i * width : (i + 1) * width]
                high = piece.astype(BF16).astype(F32)
                sums = [high + (piece - high).astype(BF16).astype(F32)]
                start = first_tap_row + index // tiles * 16
                place = slice(index % tiles * width, (index % tiles + 1) * width)
                for edge in edges:
                    block = edge[start : start + 16, place].astype(F32)
                    sums.append(block[:4] + block[4:8])
                while len(sums) > 1:
                    sums = [sums[n] + sums[n + 1] for n in range(0, len(sums), 2)]
                column = columns[t % 3]
                tap_outs[t % 3][:, column : column + width] = sums[0]
                columns[t % 3] += width
                index += 1


def place_states(sources, ranks, taps, sent, received, columns):
    requests = sources.shape[0]
    heads, width = sent.shape[1], sent.shape[2]
    parts = len(received) + 1
    depth = received[0].shape[1]
    capacity = sent.shape[0] // parts
    down, across = state_shape(depth, heads, width)
    high = capacity * down * width
    edge = columns + high
    tail = received[0].shape[0] - edge
    together = 4 if requests % 4 == 0 else 1
    sizes = [sum(x.shape[1] for x in taps[t::3]) for t in range(3)]

    def part_of(start, count):
        return pl.BlockSpec((count, depth), lambda r, *_: (start // count, 0))

    return pl.pallas_call(
        functools.partial(place_kernel, (down, across), 0, len(taps)),
        grid_spec=pltpu.PrefetchScalarGridSpec(
            num_scalar_prefetch=2,
            grid=(requests // together,),
            in_specs=[whole(x) for x in taps]
            + [pl.BlockSpec((capacity, heads, width, width), lambda r, *_: (0, 0, 0, 0))]
            + [part_of(columns, high)] * (parts - 1)
            + [part_of(edge, tail)] * (parts - 1),
            out_specs=[pl.BlockSpec((together, heads, width, width), lambda r, *_: (r, 0, 0, 0))]
            + [pl.BlockSpec((taps[0].shape[0], n), lambda r, *_: (0, 0)) for n in sizes],
        ),
        out_shape=[jax.ShapeDtypeStruct((requests, heads, width, width), F32)]
        + [jax.ShapeDtypeStruct((taps[0].shape[0], n), F32) for n in sizes],
        compiler_params=pltpu.CompilerParams(vmem_limit_bytes=40 << 20),
        cost_estimate=cost(1 << 20, 4 << 20),
        name="place_states",
    )(sources, ranks, *taps, sent, *received, *received)


def slot_plan(slot_map, all_slots, me, parts):
    requests = slot_map.shape[0]
    capacity = max(1, requests // parts)
    owners = all_slots // requests
    request_ids = jnp.arange(all_slots.shape[0], dtype=jnp.int32)
    earlier = (
        (request_ids[:, None] > request_ids[None, :])
        & (request_ids[:, None] // requests == request_ids[None, :] // requests)
        & (owners[:, None] == owners[None, :])
    )
    ranks = jnp.sum(earlier.astype(jnp.int32), axis=1)
    hops = jnp.bitwise_xor(owners, request_ids // requests)
    places = lax.dynamic_slice_in_dim(hops * capacity + ranks, me * requests, requests)
    own_slots = me * requests + jnp.arange(requests, dtype=jnp.int32)
    matches = (all_slots[None, :] == own_slots[:, None]).astype(jnp.int32)
    sources = jnp.sum(matches * hops[None, :], axis=1)
    source_ranks = jnp.sum(matches * ranks[None, :], axis=1)
    return places, sources, source_ranks, capacity


def swap(array, axis, parts, hop):
    return lax.ppermute(array, axis, [(i, i ^ hop) for i in range(parts)])


def along(array, parts, hop):
    chips = parts // 2
    pairs = [(2 * z + c, 2 * ((z + hop) % chips) + c) for z in range(chips) for c in range(2)]
    return lax.ppermute(array, "tensor", pairs)


def body(
    hidden, w_query, w_key, w_value, conv_query, conv_key, conv_value, decay_log, beta_gate,
    init_state, grad_out, state_grad_in, rollout_lengths, slot_map,
):
    parts, spread = lax.axis_size("batch"), lax.axis_size("tensor")
    chips = spread // 2
    me, mine = lax.axis_index("batch"), lax.axis_index("tensor")
    chip, core = mine // 2, mine % 2
    requests = rollout_lengths.shape[0]
    size = hidden.shape[0] // requests
    heads, width = init_state.shape[1], init_state.shape[2]
    chunks = [requests // 2, requests - requests // 2]
    starts = [sum(chunks[:i]) for i in range(len(chunks))]

    shard = hidden[: chunks[0] * size]
    rest = hidden[chunks[0] * size :]
    blocks = [shard] + [along(shard, spread, hop) for hop in range(1, chips)]
    all_slots = lax.all_gather(slot_map, "batch", axis=0, tiled=True)
    places, sources, ranks, capacity = slot_plan(slot_map, all_slots, me, parts)
    rest, blocks, places, sources, ranks = lax.optimization_barrier(
        (rest, blocks, places, sources, ranks)
    )
    blocks = blocks + [swap(x, "tensor", spread, 1) for x in blocks]
    chip_steps = jnp.arange(chips, dtype=jnp.int32)
    came = (chip - chip_steps) % chips * 2
    indices = jnp.concatenate([came + core, came + 1 - core])
    hop_order = jnp.bitwise_xor(me, jnp.array([*range(1, parts), 0], jnp.int32))
    gathered = [
        assemble(indices, blocks), lax.all_gather(rest, "tensor", axis=1, tiled=True),
    ]

    def by_head(array):
        return array.reshape(requests, size, heads).transpose(0, 2, 1)

    sent_shape = (parts * capacity, heads, width, width)
    taps = [conv_query, conv_key, conv_value]
    weights = [w_query, w_key, w_value]
    key_heads = w_query.shape[1] // width
    widths = (width, width, heads // key_heads * width)
    out, hidden_rows, pieces, decays, betas, first_grads = None, [], [], [], [], None
    for i, (start, count) in enumerate(zip(starts, chunks)):
        proj = [
            jnp.dot(gathered[i], w, preferred_element_type=F32).astype(BF16) for w in weights
        ]
        last = i == len(chunks) - 1
        sets = [range(g, g + 1) for g in range(key_heads)] if last else [range(key_heads)]
        grads, tap_sums, chunk_decays, chunk_betas = [], [], [], []
        earlier = out
        for members in sets:
            together = max(
                n for n in (1, 2, 4)
                if n * len(members) <= 4 and count % n == 0 and start % n == 0
            )
            before = None if out is None else [*earlier[:8], out[8]]
            out = core_call(
                together, start, count, members, proj, taps, by_head(decay_log),
                by_head(beta_gate), init_state, grad_out, state_grad_in, rollout_lengths,
                places, sent_shape, before,
            )
            grads.append(out[:3])
            tap_sums += out[3:6]
            chunk_decays.append(out[6])
            chunk_betas.append(out[7])
            if last:
                g = members[0]
                extra = (tap_sums, out[8]) if g == key_heads - 1 else ()
                local = weight_blocks(
                    hop_order, gathered, [earlier[:3], out[:3]], g, widths, *extra
                )
                pieces.append(
                    [local[-1]]
                    + [swap(local[hop - 1], "batch", parts, hop) for hop in range(1, parts)]
                )
        decays.append(jnp.concatenate(chunk_decays, axis=1))
        betas.append(jnp.concatenate(chunk_betas, axis=1))
        term = head_terms(spread, grads, weights)
        term = term.reshape(-1, term.shape[2])
        hidden_rows.append(lax.psum_scatter(term, "tensor", scatter_dimension=0, tiled=True))
    slot_state_grad, *grad_taps = place_states(
        sources, ranks, tap_sums, out[8], pieces[-1][1:], sum(widths)
    )
    grad_w = finish_weights(pieces, widths)
    grad_w, hidden_rows = lax.optimization_barrier((grad_w, hidden_rows))
    grad_hidden = jnp.concatenate(hidden_rows, axis=0)
    return (
        grad_hidden, *grad_w, *grad_taps, jnp.concatenate(decays), jnp.concatenate(betas),
        slot_state_grad,
    )


def solution(mesh):
    placed = (
        P("batch", "tensor"),
        P(None, "tensor"),
        P(None, "tensor"),
        P(None, "tensor"),
        P(None, "tensor"),
        P(None, "tensor"),
        P(None, "tensor"),
        P("batch", "tensor"),
        P("batch", "tensor"),
        P("batch", "tensor", None, None),
        P("batch", "tensor"),
        P("batch", "tensor", None, None),
        P("batch"),
        P("batch"),
    )
    return jax.shard_map(
        body,
        mesh=mesh,
        in_specs=placed,
        out_specs=(
            P("batch", "tensor"),
            P("batch", "tensor"),
            P("batch", "tensor"),
            P("batch", "tensor"),
            P(None, "tensor"),
            P(None, "tensor"),
            P(None, "tensor"),
            P("batch", "tensor"),
            P("batch", "tensor"),
            P("batch", "tensor", None, None),
        ),
        check_vma=False,
    )
```

```python
import functools
import jax
import jax.numpy as jnp
from jax import lax
from jax.experimental import pallas as pl
from jax.experimental.pallas import tpu as pltpu
from jax.sharding import PartitionSpec as P

EPSILON = 1e-06
F32 = jnp.float32
BF16 = jnp.bfloat16
NN = (((1,), (0,)), ((), ()))
NT = (((1,), (1,)), ((), ()))
TN = (((0,), (0,)), ((), ()))


def dot(a, b, dims=NN):
    return lax.dot_general(a.astype(BF16), b.astype(BF16), dims, preferred_element_type=F32)


def exact_dot(a, b, dims=NN):
    return lax.dot_general(
        a, b, dims, preferred_element_type=F32, precision=lax.Precision.HIGHEST
    )


def shift_down(x, count, rows):
    return jnp.where(rows >= count, pltpu.roll(x, count, 0), 0.0)


def shift_up(x, count, rows):
    size = x.shape[0]
    return jnp.where(rows < size - count, pltpu.roll(x, size - count, 0), 0.0)


def unit_lower_inverse(couplings, rows, cols):
    size = rows.shape[0]
    one = (rows == cols).astype(F32)
    first = (rows % 2 == 1) & (cols == rows - 1)
    inverses = [one - jnp.where(first, a, 0.0) for a in couplings]
    couplings = [a.astype(BF16) for a in couplings]
    block = 2
    while block < min(8, size):
        mask = ((rows // block) % 2 == 1) & (cols // block == rows // block - 1)
        inner = [dot(t, a) for t, a in zip(inverses, couplings)]
        inner = [jnp.where(mask, x, 0.0) for x in inner]
        inverses = [t - dot(x, t) for t, x in zip(inverses, inner)]
        block *= 2
    while block < size:
        count = size // (2 * block)
        half_rows = lax.broadcasted_iota(jnp.int32, (size // 2, size), 0)
        half_cols = lax.broadcasted_iota(jnp.int32, (size // 2, size), 1)
        mask = half_cols // block == 2 * (half_rows // block)
        odd = [
            jnp.concatenate(
                [t[(2 * i + 1) * block : (2 * i + 2) * block] for i in range(count)], axis=0
            )
            for t in inverses
        ]
        inner = [jnp.where(mask, dot(o, a), 0.0) for o, a in zip(odd, couplings)]
        odd = [o - dot(x, t) for o, x, t in zip(odd, inner, inverses)]
        inverses = [
            jnp.concatenate(
                [
                    piece
                    for i in range(count)
                    for piece in (
                        t[2 * i * block : (2 * i + 1) * block],
                        o[i * block : (i + 1) * block],
                    )
                ],
                axis=0,
            )
            for t, o in zip(inverses, odd)
        ]
        block *= 2
    return inverses


def core_kernel(first_request, first_head, together, key_heads, later, *refs):
    lengths, places = refs[:2]
    proj, taps, (decay, beta, init_state, grad_out, state_grad) = refs[2:5], refs[5:8], refs[8:13]
    refs = refs[13:]
    if later:
        old_taps, refs = refs[:3], refs[3 + key_heads :]
    grads, grad_taps = refs[:3], refs[3:6]
    grad_decay, grad_beta = refs[6:8]
    sent, (held, sem) = refs[8:-2], refs[-2:]
    step = pl.program_id(0)
    width = init_state.shape[-1]
    size = proj[0].shape[0] // together
    heads = init_state.shape[1]
    group = heads // key_heads
    rows = lax.broadcasted_iota(jnp.int32, (size, size), 0)
    cols = lax.broadcasted_iota(jnp.int32, (size, size), 1)
    wide_rows = lax.broadcasted_iota(jnp.int32, (size, width), 0)
    causal = rows >= cols
    strict = rows > cols
    lower = causal.astype(F32)
    upper = (rows <= cols).astype(F32)
    one = (rows == cols).astype(F32)

    units = [(r, g) for r in range(together) for g in range(key_heads)]
    pairs = [(r, h) for r in range(together) for h in range(heads)]
    unit_of = {(r, h): r * key_heads + h // group for r, h in pairs}
    spans = [slice(r * size, (r + 1) * size) for r in range(together)]
    request = [first_request + step * together + r for r in range(together)]
    length = [lengths[x] for x in request]
    live_row = [
        (lax.broadcasted_iota(jnp.int32, (heads, size), 1) < n).astype(F32) for n in length
    ]
    live_col = [
        (lax.broadcasted_iota(jnp.int32, (size, heads), 0) < n).astype(F32) for n in length
    ]
    live_wide = [(wide_rows < n).astype(F32) for n in length]
    picked = slice(first_head, first_head + heads)
    gate_row = [decay[r, picked, :] * live_row[r] for r in range(together)]
    rate_row = [beta[r, picked, :] * live_row[r] for r in range(together)]
    cum_row = [exact_dot(x, lower, NT) for x in gate_row]
    cum_col = [exact_dot(lower, x, NT) for x in gate_row]
    rate_col = [exact_dot(one, x, NT) for x in rate_row]
    growth_col = [jnp.exp(x) for x in cum_col]

    def prepare(r, kind, index):
        cut = slice(index * width, (index + 1) * width)
        x = proj[kind][spans[r], cut].astype(F32)
        mixed = x * taps[kind][3:4, cut]
        for i in range(3):
            mixed = mixed + shift_down(x, 3 - i, wide_rows) * taps[kind][i : i + 1, cut]
        gate = 1.0 / (1.0 + jnp.exp(-mixed))
        active = mixed * gate
        return active, gate + active * (1.0 - gate)

    def unit(active, factor):
        total = jnp.sum(active * active, axis=-1, keepdims=True) + EPSILON
        scale = factor * lax.rsqrt(total)
        return active * scale, scale, 1.0 / total

    q_in = [prepare(r, 0, g) for r, g in units]
    k_in = [prepare(r, 1, g) for r, g in units]
    v_in = [prepare(r, 2, h) for r, h in pairs]
    q_unit = [unit(x[0], width ** (-0.5)) for x in q_in]
    k_unit = [unit(x[0], 1.0) for x in k_in]
    q_f = [x[0] for x in q_unit]
    k_f = [x[0] for x in k_unit]
    q_b = [x.astype(BF16) for x in q_f]
    k_b = [x.astype(BF16) for x in k_f]
    kk = [dot(k, k, NT) for k in k_b]
    qk = [dot(q, k, NT) for q, k in zip(q_b, k_b)]
    kq = [dot(k, q, NT) for q, k in zip(q_b, k_b)]

    every = range(len(pairs))
    of = [unit_of[p] for p in pairs]
    cum_c = [cum_col[r][:, h : h + 1] for r, h in pairs]
    cum_r = [cum_row[r][h : h + 1, :] for r, h in pairs]
    rate = [rate_col[r][:, h : h + 1] for r, h in pairs]
    growth = [growth_col[r][:, h : h + 1] for r, h in pairs]
    last = [x[:, size - 1 :] for x in cum_r]
    final = [jnp.exp(x) for x in last]
    rest = [jnp.exp(last[i] - cum_c[i]) for i in every]
    within = [jnp.exp(jnp.where(causal, cum_c[i] - cum_r[i], -jnp.inf)) for i in every]
    within_t = [jnp.exp(jnp.where(rows <= cols, cum_r[i] - cum_c[i], -jnp.inf)) for i in every]
    couplings = [jnp.where(strict, rate[i] * kk[of[i]] * within[i], 0.0) for i in every]
    inverses = [t.astype(BF16) for t in unit_lower_inverse(couplings, rows, cols)]

    s_b = [init_state[r, h].astype(BF16) for r, h in pairs]
    ds_b = [state_grad[r, h].astype(BF16) for r, h in pairs]
    k_s = [dot(k_b[of[i]], s_b[i]) for i in every]
    left = [v_in[i][0] - growth[i] * k_s[i] for i in every]
    new_b = [dot(inverses[i], rate[i] * left[i]).astype(BF16) for i in every]
    out_b = [
        (grad_out[spans[r], h * width : (h + 1) * width].astype(F32) * live_wide[r]).astype(BF16)
        for r, h in pairs
    ]
    d_new = [
        dot(kq[of[i]] * within_t[i], out_b[i]) + rest[i] * dot(k_b[of[i]], ds_b[i]) for i in every
    ]
    d_right = [dot(inverses[i], d_new[i], TN) for i in every]
    d_scores = [dot(out_b[i], new_b[i], NT) * within[i] for i in every]
    d_coup = [
        jnp.where(strict, -dot(d_right[i], new_b[i], NT) * within[i], 0.0) for i in every
    ]
    back_b = [(-(rate[i] * growth[i]) * d_right[i]).astype(BF16) for i in every]
    u_q = [growth[i] * dot(out_b[i], s_b[i], NT) for i in every]
    u_k = [dot(back_b[i], s_b[i], NT) for i in every]
    u_e = [rest[i] * dot(new_b[i], ds_b[i], NT) for i in every]

    def leave(r):
        place = places[first_request + step * together + r]
        return [
            pltpu.make_async_copy(
                held.at[r, pl.ds(g * group, group)], sent[g].at[place], sem.at[r, g]
            )
            for g in range(key_heads)
        ]

    @pl.when(step > 0)
    def _():
        for r in range(together):
            for copy in leave(r):
                copy.wait()

    cum_from_rows, cum_from_cols, rate_grads, last_grads = [], [], [], []
    for i, (r, h) in enumerate(pairs):
        u = of[i]
        y = d_coup[i] * kk[u]
        y_row = jnp.sum(y, axis=-1, keepdims=True)
        scored = d_scores[i] * qk[u]
        ended = jnp.sum(k_f[u] * u_e[i], axis=-1, keepdims=True)
        rate_grads.append(jnp.sum(d_right[i] * left[i], axis=-1, keepdims=True) + y_row)
        direct = q_f[u] * u_q[i] + k_f[u] * u_k[i] + scored
        cum_from_rows.append(jnp.sum(direct, axis=-1, keepdims=True) + rate[i] * y_row - ended)
        cum_from_cols.append(jnp.sum(scored + rate[i] * y, axis=0, keepdims=True))
        carried = jnp.sum(state_grad[r, h] * init_state[r, h], axis=0, keepdims=True)
        last_grads.append(
            jnp.sum(ended, axis=0, keepdims=True)
            + final[i] * jnp.sum(carried, axis=1, keepdims=True)
        )
        held[r, h] = (
            final[i] * state_grad[r, h]
            + dot(q_b[u], growth[i] * out_b[i].astype(F32), TN)
            + dot(k_b[u], back_b[i], TN)
        ).astype(BF16)
    for r in range(together):
        for copy in leave(r):
            copy.start()
    for r in range(together):
        mine = [i for i in every if pairs[i][0] == r]
        gate_grad = exact_dot(upper, jnp.concatenate([cum_from_rows[i] for i in mine], axis=1))
        gate_grad = gate_grad - exact_dot(
            upper, jnp.concatenate([cum_from_cols[i] for i in mine], axis=0), NT
        )
        gate_grad = gate_grad + jnp.concatenate([last_grads[i] for i in mine], axis=1)
        grad_decay[spans[r], :] = gate_grad * live_col[r]
        grad_beta[spans[r], :] = (
            jnp.concatenate([rate_grads[i] for i in mine], axis=1) * live_col[r]
        )

    @pl.when(step == 0)
    def _():
        for i, grad_tap in enumerate(grad_taps):
            grad_tap[...] = old_taps[i][...] if later else jnp.zeros_like(grad_tap)

    def conv_back(d_active, slope, r, kind, index):
        cut = slice(index * width, (index + 1) * width)
        x = proj[kind][spans[r], cut].astype(F32)
        d_mixed = d_active * slope
        d_x = d_mixed * taps[kind][3:4, cut]
        sums = []
        for i in range(3):
            moved = shift_up(d_mixed, 3 - i, wide_rows)
            d_x = d_x + moved * taps[kind][i : i + 1, cut]
            sums.append(jnp.sum(moved * x, axis=0, keepdims=True))
        sums.append(jnp.sum(d_mixed * x, axis=0, keepdims=True))
        grads[kind][spans[r], cut] = d_x.astype(BF16)
        grad_taps[kind][:, cut] += jnp.concatenate(sums, axis=0)

    def unit_back(d_unit, unit_in, active):
        unit_rows, scale, inverse_total = unit_in
        inner = jnp.sum(d_unit * active, axis=-1, keepdims=True)
        return scale * (d_unit - active * (inner * inverse_total))

    for u, (r, g) in enumerate(units):
        members = [i for i in every if of[i] == u]
        scores_sum = sum(d_scores[i] for i in members).astype(BF16)
        kk_sum = sum(rate[i] * d_coup[i] for i in members)
        kk_sum = (kk_sum + kk_sum.T).astype(BF16)
        d_q = sum(u_q[i] for i in members) + dot(scores_sum, k_b[u])
        d_k = sum(u_k[i] + u_e[i] for i in members)
        d_k = d_k + dot(scores_sum, q_b[u], TN) + dot(kk_sum, k_b[u])
        conv_back(unit_back(d_q, q_unit[u], q_in[u][0]), q_in[u][1], r, 0, g)
        conv_back(unit_back(d_k, k_unit[u], k_in[u][0]), k_in[u][1], r, 1, g)
    for i, (r, h) in enumerate(pairs):
        conv_back(rate[i] * d_right[i], v_in[i][1], r, 2, h)

    @pl.when(step == pl.num_programs(0) - 1)
    def _():
        for r in range(together):
            for copy in leave(r):
                copy.wait()


def core_call(
    together, first, count, members, proj, taps, decay, beta, init_state, grad_out, state_grad,
    lengths, places, sent_shape, before,
):
    all_heads, width = init_state.shape[1:3]
    size = decay.shape[2]
    key_heads = len(members)
    heads = key_heads * (all_heads * width // proj[0].shape[1])
    part = members[0] // key_heads
    first_head = part * heads
    widths = [key_heads * width, key_heads * width, heads * width]
    rows = count * size
    start = first // together

    def here(offset, column, columns):
        return pl.BlockSpec((together * size, columns), lambda i, *_: (offset + i, column))

    def fixed(array, column, columns):
        return pl.BlockSpec((array.shape[0], columns), lambda i, *_: (0, column))

    by_request = pl.BlockSpec((together, all_heads, size), lambda i, *_: (start + i, 0, 0))
    state = pl.BlockSpec((together, heads, width, width), lambda i, *_: (start + i, part, 0, 0))
    small = pl.BlockSpec((together * size, heads), lambda i, *_: (i, 0))
    anywhere = pl.BlockSpec(memory_space=pl.ANY)
    kept = [] if before is None else [*before[3:6], *[before[8 + g] for g in members]]
    kept_columns = [part if x.shape[1] > n else 0 for x, n in zip(kept, widths)]
    products = count * heads * 26 * 2 * size * width * width
    return pl.pallas_call(
        functools.partial(core_kernel, first, first_head, together, key_heads, bool(kept)),
        grid_spec=pltpu.PrefetchScalarGridSpec(
            num_scalar_prefetch=2,
            grid=(count // together,),
            in_specs=[here(0, part, n) for n in widths]
            + [fixed(x, part, n) for x, n in zip(taps, widths)]
            + [by_request, by_request, state, here(start, part, heads * width), state]
            + [fixed(x, j, n) for x, j, n in zip(kept, kept_columns, widths)]
            + [anywhere] * (key_heads if kept else 0),
            out_specs=[here(0, 0, n) for n in widths]
            + [fixed(x, 0, n) for x, n in zip(taps, widths)]
            + [small, small] + [anywhere] * key_heads,
            scratch_shapes=[
                pltpu.VMEM((together, heads, width, width), BF16),
                pltpu.SemaphoreType.DMA((together, key_heads)),
            ],
        ),
        out_shape=[jax.ShapeDtypeStruct((rows, n), BF16) for n in widths]
        + [jax.ShapeDtypeStruct((x.shape[0], n), F32) for x, n in zip(taps, widths)]
        + [jax.ShapeDtypeStruct((rows, heads), F32)] * 2
        + [jax.ShapeDtypeStruct(sent_shape, BF16)] * key_heads,
        input_output_aliases={16 + g: 8 + g for g in range(key_heads)} if kept else {},
        compiler_params=pltpu.CompilerParams(vmem_limit_bytes=50 << 20),
        cost_estimate=cost(12 * products, count * heads * 400000),
        name="core_grads",
    )(
        lengths, places, *proj, *taps, decay, beta, init_state, grad_out, state_grad, *kept
    )


COST = 10**9
FINISH = 15 * 10**9


def whole(array):
    return pl.BlockSpec(array.shape, lambda *_: (0,) * len(array.shape))


def cost(flops, size):
    return pl.CostEstimate(flops=flops // COST, bytes_accessed=size // COST, transcendentals=0)


def assemble_kernel(indices, *refs):
    blocks, features = refs[:-1], refs[-1]
    width = blocks[0].shape[1]
    for i, block in enumerate(blocks):
        features[:, pl.ds(pl.multiple_of(indices[i] * width, width), width)] = block[...]


def assemble(indices, blocks):
    rows, width = blocks[0].shape
    tile = 128

    def tiles(count):
        return pl.BlockSpec((tile, count), lambda i, *_: (i, 0))

    return pl.pallas_call(
        assemble_kernel,
        grid_spec=pltpu.PrefetchScalarGridSpec(
            num_scalar_prefetch=1,
            grid=(rows // tile,),
            in_specs=[tiles(width)] * len(blocks),
            out_specs=tiles(width * len(blocks)),
        ),
        out_shape=jax.ShapeDtypeStruct((rows, width * len(blocks)), BF16),
        compiler_params=pltpu.CompilerParams(vmem_limit_bytes=32 << 20),
        cost_estimate=cost(1, 4 << 20),
        name="assemble",
    )(indices, *blocks)


def term_kernel(sets, *refs):
    grads, weights, (out, held) = refs[: 3 * sets], refs[3 * sets : 3 * sets + 3], refs[-2:]
    width = out.shape[2]

    @pl.when(pl.program_id(0) == 0)
    def _():
        column = 0
        for kind in range(3):
            for g in range(sets):
                grad = grads[3 * g + kind]
                held[:, column : column + grad.shape[1]] = grad[...]
                column += grad.shape[1]

    total, column = 0.0, 0
    for weight in weights:
        total = total + dot(held[:, column : column + weight.shape[1]], weight[...], NT)
        column += weight.shape[1]
    for i in range(out.shape[0]):
        out[i] = total[:, i * width : (i + 1) * width].astype(BF16)


def head_terms(parts, sets, weights):
    rows = sets[0][0].shape[0]
    depth = weights[0].shape[0]
    columns = sum(w.shape[1] for w in weights)
    width = depth // parts
    tile = max(1, 512 // width)
    grads = [x for group in sets for x in group]
    return pl.pallas_call(
        functools.partial(term_kernel, len(sets)),
        grid=(parts // tile,),
        in_specs=[whole(x) for x in grads]
        + [pl.BlockSpec((tile * width, w.shape[1]), lambda i: (i, 0)) for w in weights],
        out_specs=pl.BlockSpec((tile, rows, width), lambda i: (i, 0, 0)),
        out_shape=jax.ShapeDtypeStruct((parts, rows, width), BF16),
        scratch_shapes=[pltpu.VMEM((rows, columns), BF16)],
        compiler_params=pltpu.CompilerParams(vmem_limit_bytes=50 << 20),
        cost_estimate=cost(2 * rows * depth * columns, 7 << 20),
        name="head_terms",
    )(*grads, *weights)


def weight_kernel(parts, chunks, plan, order, *refs):
    features, grads = refs[:chunks], refs[chunks : 4 * chunks]
    taps, states = refs[4 * chunks : 4 * chunks + 3], refs[4 * chunks + 3]
    outs, turned = refs[4 * chunks + 4 : -1], refs[-1]
    step = pl.program_id(0)
    starts = [sum(x.shape[0] for x in features[:i]) for i in range(chunks)]
    width = states.shape[2]

    @pl.when(step == 0)
    def _():
        for c, start in enumerate(starts):
            row = 0
            for grad in grads[3 * c : 3 * c + 3]:
                count, columns = grad.shape
                turned[row : row + columns, start : start + count] = grad[...].T
                row += columns
        for index, row, hop in plan["states"]:
            for t in range(states.shape[0] // parts * states.shape[1]):
                slot, head = divmod(t, states.shape[1])
                tall, wide = divmod(t, outs[index].shape[1] // width)
                outs[index][
                    row + tall * width : row + (tall + 1) * width, wide * width : (wide + 1) * width
                ] = states[hop * (states.shape[0] // parts) + slot, head]
        for index, row in plan["taps"]:
            store_taps(outs[index], row, tap_pieces(taps, width))

    total = sum(
        dot(turned[:, start : start + x.shape[0]], x[...]) for start, x in zip(starts, features)
    )
    for hop, pieces in plan["weights"]:

        @pl.when(step == plan["hops"].index(hop))
        def _():
            for index, row, low, high in pieces:
                outs[index][row : row + high - low, :] = total[low:high].astype(outs[index].dtype)


def tap_pieces(taps, width):
    return [x[:, i * width : (i + 1) * width] for x in taps for i in range(x.shape[1] // width)]


def store_taps(out, row, pieces):
    width = pieces[0].shape[1]
    across = out.shape[1] // width
    for index, piece in enumerate(pieces):
        high = piece.astype(BF16).astype(F32)
        block = jnp.concatenate([high, piece - high], axis=0)
        block = jnp.concatenate([block, jnp.zeros_like(block)], axis=0).astype(BF16)
        start = row + index // across * 16
        out[start : start + 16, index % across * width : (index % across + 1) * width] = block


def load_taps(source, row, count, width):
    across = source.shape[1] // width
    pieces = []
    for index in range(count):
        start = row + index // across * 16
        block = source[start : start + 16, index % across * width : (index % across + 1) * width]
        block = block.astype(F32)
        pieces.append(block[:4] + block[4:8])
    return pieces


def rounded_taps(pieces):
    highs = [piece.astype(BF16).astype(F32) for piece in pieces]
    return [high + (piece - high).astype(BF16).astype(F32) for piece, high in zip(pieces, highs)]


def weight_plan(parts, columns, depth, states, pieces):
    width = states.shape[2]
    tiles = states.shape[0] // parts * states.shape[1]
    state_rows = -(-tiles // (depth // width)) * width
    tap_rows = -(-pieces // (depth // width)) * 16
    if parts == 4:
        half = columns // 2
        plan = {
            "hops": [3, 1, 2, 0],
            "weights": [
                (3, [(0, half, 0, half), (1, half, half, columns)]),
                (1, [(0, 0, 0, half), (3, 0, half, columns)]),
                (2, [(1, 0, half, columns), (2, 0, 0, half)]),
                (0, [(4, 0, 0, columns)]),
            ],
            "states": [
                (0, columns, 1), (0, columns + state_rows, 3), (1, columns, 2),
            ],
            "taps": [(0, columns + 2 * state_rows)],
        }
        shapes = [
            ((columns + 2 * state_rows + tap_rows, depth), BF16),
            ((columns + state_rows, depth), BF16),
            ((half, depth), F32),
            ((half, depth), F32),
            ((columns, depth), F32),
        ]
    else:
        hops = [*range(1, parts), 0]
        plan = {
            "hops": hops,
            "weights": [(hop, [(i, 0, 0, columns)]) for i, hop in enumerate(hops)],
            "states": [(i, columns, hop) for i, hop in enumerate(hops[:-1])],
            "taps": [(i, columns + state_rows) for i in range(parts - 1)],
        }
        shapes = [((columns + state_rows + tap_rows, depth), BF16)] * (parts - 1)
        shapes.append(((columns, depth), F32))
    return plan, [jax.ShapeDtypeStruct(*x) for x in shapes], state_rows, tap_rows


def weight_blocks(me, parts, plan, shapes, features, grads, index, widths, taps, states):
    depth = features[0].shape[1] // parts
    columns = sum(widths)
    rows = sum(x.shape[0] for x in features)
    order = jnp.bitwise_xor(me, jnp.array(plan["hops"], jnp.int32))

    def of_key_head(array, width):
        place = index if array.shape[1] > width else 0
        return pl.BlockSpec((array.shape[0], width), lambda i, order: (0, place))

    return pl.pallas_call(
        functools.partial(weight_kernel, parts, len(features), plan),
        grid_spec=pltpu.PrefetchScalarGridSpec(
            num_scalar_prefetch=1,
            grid=(parts,),
            in_specs=[
                pl.BlockSpec((x.shape[0], depth), lambda i, order: (0, order[i]))
                for x in features
            ]
            + [of_key_head(x, n) for group in grads for x, n in zip(group, widths)]
            + [whole(x) for x in (*taps, states)],
            out_specs=[whole(x) for x in shapes],
            scratch_shapes=[pltpu.VMEM((columns, rows), BF16)],
        ),
        out_shape=shapes,
        compiler_params=pltpu.CompilerParams(vmem_limit_bytes=50 << 20),
        cost_estimate=cost(2 * rows * depth * parts * columns, 8 << 20),
        name="weight_blocks",
    )(order, *features, *[x for group in grads for x in group], *taps, states)


def middle_kernel(half, state_rows, *refs):
    first, second, kept_first, kept_second = refs[:4]
    taps, (next_first, next_second) = refs[4:7], refs[7:]
    columns, width = 2 * half, taps[0].shape[1]
    next_first[:half, :] = (kept_first[...] + first[half:columns, :].astype(F32)).astype(BF16)
    next_second[...] = (kept_second[...] + second[half:columns, :].astype(F32)).astype(BF16)
    start = columns + state_rows
    next_first[half : half + state_rows, :] = first[start : start + state_rows, :]
    mine = rounded_taps(tap_pieces(taps, width))
    theirs = load_taps(first, columns + 2 * state_rows, len(mine), width)
    store_taps(next_first, half + state_rows, [a + b for a, b in zip(mine, theirs)])


def exchange(arrays, taps, parts, columns, state_rows, tap_rows):
    if parts != 4:
        return [swap(x, "batch", parts, hop + 1) for hop, x in enumerate(arrays[:-1])]
    half, depth = columns // 2, arrays[0].shape[1]
    first, second = swap(arrays[0], "batch", parts, 1), swap(arrays[1], "batch", parts, 2)
    shapes = [
        jax.ShapeDtypeStruct((half + state_rows + tap_rows, depth), BF16),
        jax.ShapeDtypeStruct((half, depth), BF16),
    ]
    inputs = [first, second, arrays[2], arrays[3], *taps]
    next_first, next_second = pl.pallas_call(
        functools.partial(middle_kernel, half, state_rows),
        grid=(1,),
        in_specs=[whole(x) for x in inputs],
        out_specs=[whole(x) for x in shapes],
        out_shape=shapes,
        compiler_params=pltpu.CompilerParams(vmem_limit_bytes=40 << 20),
        cost_estimate=cost(1, 1),
        name="pass_on",
    )(*inputs)
    return [first, second, next_first, next_second]


def second_exchange(arrays, parts):
    if parts != 4:
        return arrays
    return [*arrays[:2], swap(arrays[2], "batch", parts, 2), swap(arrays[3], "batch", parts, 1)]


def finish_kernel(parts, sources, widths, *refs):
    outs = refs[-3:]
    columns = sum(widths)
    half = columns // 2
    for g in range((len(refs) - 3) // (sources + 1)):
        own, *pieces = refs[g * (sources + 1) : (g + 1) * (sources + 1)]
        if parts == 4:
            upper = own[:half] + (pieces[0][...].astype(F32) + pieces[2][...].astype(F32))
            lower = own[half:] + (pieces[1][...].astype(F32) + pieces[3][...].astype(F32))
            total = jnp.concatenate([upper.T, lower.T], axis=1)
        else:
            total = sum((piece[...].astype(F32) for piece in pieces), own[...]).T
        start = 0
        for out, width in zip(outs, widths):
            out[:, g * width : (g + 1) * width] = total[:, start : start + width]
            start += width


def finish_weights(parts, own, pieces, widths):
    key_heads, rows, columns = len(pieces), own[0].shape[1], sum(widths)
    tile = min(rows, 128)
    sizes = [key_heads * n for n in widths]
    count = columns // 2 if parts == 4 else columns
    specs = [pl.BlockSpec((columns, tile), lambda i: (0, i))]
    specs += [pl.BlockSpec((count, tile), lambda i: (0, i))] * len(pieces[0])
    return pl.pallas_call(
        functools.partial(finish_kernel, parts, len(pieces[0]), widths),
        grid=(rows // tile,),
        in_specs=specs * key_heads,
        out_specs=[pl.BlockSpec((tile, n), lambda i: (i, 0)) for n in sizes],
        out_shape=[jax.ShapeDtypeStruct((rows, n), F32) for n in sizes],
        compiler_params=pltpu.CompilerParams(vmem_limit_bytes=32 << 20),
        cost_estimate=pl.CostEstimate(flops=FINISH, bytes_accessed=1, transcendentals=0),
        name="finish_weights",
    )(*[x for mine, group in zip(own, pieces) for x in (mine, *group)])


def place_kernel(parts, key_heads, columns, state_rows, sources, ranks, *refs):
    taps, kept = refs[: 3 * key_heads], refs[3 * key_heads : 4 * key_heads]
    count = (len(refs) - 4) // key_heads - 4
    received = refs[4 * key_heads : -4]
    out, tap_outs = refs[-4], refs[-3:]
    group, width = kept[0].shape[1], kept[0].shape[2]
    step = pl.program_id(0)
    for g in range(key_heads):
        arrays = received[g * count : (g + 1) * count]
        if parts == 4:
            places = [(0, columns), (1, columns), (2, columns // 2)]
        else:
            places = [(i, columns) for i in range(parts - 1)]
        across = arrays[0].shape[1] // width
        for j in range(out.shape[0]):
            source, rank = sources[step * out.shape[0] + j], ranks[step * out.shape[0] + j]

            @pl.when(source == 0)
            def _():
                out[j, g * group : (g + 1) * group] = kept[g][rank].astype(F32)

            for hop, (index, row) in enumerate(places):
                for slot in range(kept[g].shape[0] // parts):

                    @pl.when((source == hop + 1) & (rank == slot))
                    def _():
                        for h in range(group):
                            tall, wide = divmod(slot * group + h, across)
                            start = row + tall * width
                            out[j, g * group + h] = arrays[index][
                                start : start + width, wide * width : (wide + 1) * width
                            ].astype(F32)

        @pl.when(step == 0)
        def _():
            mine = rounded_taps(tap_pieces(taps[3 * g : 3 * g + 3], width))
            n = len(mine)
            if parts == 4:
                theirs = load_taps(arrays[0], columns + 2 * state_rows, n, width)
                mine = rounded_taps([a + b for a, b in zip(mine, theirs)])
                others = [load_taps(arrays[2], columns // 2 + state_rows, n, width)]
            else:
                others = [load_taps(x, columns + state_rows, n, width) for x in arrays]
            groups = [mine, *others]
            while len(groups) > 1:
                groups = [
                    [a + b for a, b in zip(groups[i], groups[i + 1])]
                    for i in range(0, len(groups), 2)
                ]
            pieces = groups[0]
            for tap_out in tap_outs:
                total = tap_out.shape[1] // key_heads
                for i in range(total // width):
                    start = g * total + i * width
                    tap_out[:, start : start + width] = pieces.pop(0)


def place_states(parts, sources, ranks, taps, sent, pieces, columns, state_rows):
    requests, key_heads = sources.shape[0], len(sent)
    heads, width = key_heads * sent[0].shape[1], sent[0].shape[2]
    together = 4 if requests % 4 == 0 else 1
    sizes = [sum(x.shape[1] for x in taps[t::3]) for t in range(3)]
    inputs = [*taps, *sent, *[x for group in pieces for x in group]]
    return pl.pallas_call(
        functools.partial(place_kernel, parts, key_heads, columns, state_rows),
        grid_spec=pltpu.PrefetchScalarGridSpec(
            num_scalar_prefetch=2,
            grid=(requests // together,),
            in_specs=[whole(x) for x in inputs],
            out_specs=[pl.BlockSpec((together, heads, width, width), lambda r, *_: (r, 0, 0, 0))]
            + [pl.BlockSpec((taps[0].shape[0], n), lambda r, *_: (0, 0)) for n in sizes],
        ),
        out_shape=[jax.ShapeDtypeStruct((requests, heads, width, width), F32)]
        + [jax.ShapeDtypeStruct((taps[0].shape[0], n), F32) for n in sizes],
        compiler_params=pltpu.CompilerParams(vmem_limit_bytes=50 << 20),
        cost_estimate=cost(1 << 20, 4 << 20),
        name="place_states",
    )(sources, ranks, *inputs)


def slot_plan(slot_map, all_slots, me, parts):
    requests = slot_map.shape[0]
    capacity = max(1, requests // parts)
    owners = all_slots // requests
    request_ids = jnp.arange(all_slots.shape[0], dtype=jnp.int32)
    earlier = (
        (request_ids[:, None] > request_ids[None, :])
        & (request_ids[:, None] // requests == request_ids[None, :] // requests)
        & (owners[:, None] == owners[None, :])
    )
    ranks = jnp.sum(earlier.astype(jnp.int32), axis=1)
    hops = jnp.bitwise_xor(owners, request_ids // requests)
    places = lax.dynamic_slice_in_dim(hops * capacity + ranks, me * requests, requests)
    own_slots = me * requests + jnp.arange(requests, dtype=jnp.int32)
    matches = (all_slots[None, :] == own_slots[:, None]).astype(jnp.int32)
    sources = jnp.sum(matches * hops[None, :], axis=1)
    source_ranks = jnp.sum(matches * ranks[None, :], axis=1)
    return places, sources, source_ranks, capacity


def swap(array, axis, parts, hop):
    return lax.ppermute(array, axis, [(i, i ^ hop) for i in range(parts)])


def along(array, parts, hop):
    chips = parts // 2
    pairs = [(2 * z + c, 2 * ((z + hop) % chips) + c) for z in range(chips) for c in range(2)]
    return lax.ppermute(array, "tensor", pairs)


def body(
    hidden, w_query, w_key, w_value, conv_query, conv_key, conv_value, decay_log, beta_gate,
    init_state, grad_out, state_grad_in, rollout_lengths, slot_map,
):
    parts, spread = lax.axis_size("batch"), lax.axis_size("tensor")
    chips = spread // 2
    me, mine = lax.axis_index("batch"), lax.axis_index("tensor")
    chip, core = mine // 2, mine % 2
    requests = rollout_lengths.shape[0]
    size = hidden.shape[0] // requests
    heads, width = init_state.shape[1], init_state.shape[2]
    chunks = [requests // 2, requests - requests // 2]
    starts = [sum(chunks[:i]) for i in range(len(chunks))]

    shard = hidden[: chunks[0] * size]
    rest = hidden[chunks[0] * size :]
    blocks = [shard] + [along(shard, spread, hop) for hop in range(1, chips)]
    all_slots = lax.all_gather(slot_map, "batch", axis=0, tiled=True)
    places, sources, ranks, capacity = slot_plan(slot_map, all_slots, me, parts)
    rest, blocks, places, sources, ranks = lax.optimization_barrier(
        (rest, blocks, places, sources, ranks)
    )
    blocks = blocks + [swap(x, "tensor", spread, 1) for x in blocks]
    chip_steps = jnp.arange(chips, dtype=jnp.int32)
    came = (chip - chip_steps) % chips * 2
    indices = jnp.concatenate([came + core, came + 1 - core])
    gathered = [
        assemble(indices, blocks), lax.all_gather(rest, "tensor", axis=1, tiled=True),
    ]

    def by_head(array):
        return array.reshape(requests, size, heads).transpose(0, 2, 1)

    taps = [conv_query, conv_key, conv_value]
    weights = [w_query, w_key, w_value]
    key_heads = w_query.shape[1] // width
    group = heads // key_heads
    sent_shape = (parts * capacity, group, width, width)
    widths = (width, width, group * width)
    out, hidden_rows, own, pieces, decays, betas, sent = None, [], [], [], [], [], None
    for i, (start, count) in enumerate(zip(starts, chunks)):
        proj = [
            jnp.dot(gathered[i], w, preferred_element_type=F32).astype(BF16) for w in weights
        ]
        last = i == len(chunks) - 1
        sets = [range(g, g + 1) for g in range(key_heads)] if last else [range(key_heads)]
        grads, tap_sums, chunk_decays, chunk_betas = [], [], [], []
        earlier = out
        for members in sets:
            together = max(
                n for n in (1, 2, 4)
                if n * len(members) <= 4 and count % n == 0 and start % n == 0
            )
            before = earlier
            out = core_call(
                together, start, count, members, proj, taps, by_head(decay_log),
                by_head(beta_gate), init_state, grad_out, state_grad_in, rollout_lengths,
                places, sent_shape, before,
            )
            grads.append(out[:3])
            tap_sums += out[3:6]
            chunk_decays.append(out[6])
            chunk_betas.append(out[7])
            if last:
                g = members[0]
                if g == key_heads - 1:
                    term = head_terms(spread, grads, weights)
                    term, out, pieces = lax.optimization_barrier((term, out, pieces))
                states = jax.ShapeDtypeStruct(sent_shape, BF16)
                plan, shapes, state_rows, tap_rows = weight_plan(
                    parts, sum(widths), gathered[0].shape[1] // parts, states,
                    sum(widths) // width,
                )
                local = weight_blocks(
                    me, parts, plan, shapes, gathered, [earlier[:3], out[:3]], g, widths,
                    out[3:6], out[8],
                )
                if g < key_heads - 1:
                    local, proj = lax.optimization_barrier((local, proj))
                own.append(local[-1])
                pieces.append(
                    exchange(local, out[3:6], parts, sum(widths), state_rows, tap_rows)
                )
                sent = [*(sent or []), out[8]]
            elif members[-1] == key_heads - 1:
                term = head_terms(spread, grads, weights)
        decays.append(jnp.concatenate(chunk_decays, axis=1))
        betas.append(jnp.concatenate(chunk_betas, axis=1))
        term = term.reshape(-1, term.shape[2])
        hidden_rows.append(lax.psum_scatter(term, "tensor", scatter_dimension=0, tiled=True))
    pieces = [second_exchange(x, parts) for x in pieces]
    slot_state_grad, *grad_taps = place_states(
        parts, sources, ranks, tap_sums, sent, pieces, sum(widths), state_rows
    )
    grad_w = finish_weights(parts, own, pieces, widths)
    grad_w, hidden_rows = lax.optimization_barrier((grad_w, hidden_rows))
    grad_hidden = jnp.concatenate(hidden_rows, axis=0)
    return (
        grad_hidden, *grad_w, *grad_taps, jnp.concatenate(decays), jnp.concatenate(betas),
        slot_state_grad,
    )


def solution(mesh):
    placed = (
        P("batch", "tensor"),
        P(None, "tensor"),
        P(None, "tensor"),
        P(None, "tensor"),
        P(None, "tensor"),
        P(None, "tensor"),
        P(None, "tensor"),
        P("batch", "tensor"),
        P("batch", "tensor"),
        P("batch", "tensor", None, None),
        P("batch", "tensor"),
        P("batch", "tensor", None, None),
        P("batch"),
        P("batch"),
    )
    return jax.shard_map(
        body,
        mesh=mesh,
        in_specs=placed,
        out_specs=(
            P("batch", "tensor"),
            P("batch", "tensor"),
            P("batch", "tensor"),
            P("batch", "tensor"),
            P(None, "tensor"),
            P(None, "tensor"),
            P(None, "tensor"),
            P("batch", "tensor"),
            P("batch", "tensor"),
            P("batch", "tensor", None, None),
        ),
        check_vma=False,
    )
```

```python
import functools
import jax
import jax.numpy as jnp
from jax import lax
from jax.experimental import pallas as pl
from jax.experimental.pallas import tpu as pltpu
from jax.sharding import PartitionSpec as P

EPSILON = 1e-06
F32 = jnp.float32
BF16 = jnp.bfloat16
NN = (((1,), (0,)), ((), ()))
NT = (((1,), (1,)), ((), ()))
TN = (((0,), (0,)), ((), ()))


def dot(a, b, dims=NN):
    return lax.dot_general(a.astype(BF16), b.astype(BF16), dims, preferred_element_type=F32)


def exact_dot(a, b, dims=NN):
    return lax.dot_general(
        a, b, dims, preferred_element_type=F32, precision=lax.Precision.HIGHEST
    )


def shift_down(x, count, rows):
    return jnp.where(rows >= count, pltpu.roll(x, count, 0), 0.0)


def shift_up(x, count, rows):
    size = x.shape[0]
    return jnp.where(rows < size - count, pltpu.roll(x, size - count, 0), 0.0)


def unit_lower_inverse(couplings, rows, cols):
    size = rows.shape[0]
    one = (rows == cols).astype(F32)
    first = (rows % 2 == 1) & (cols == rows - 1)
    inverses = [one - jnp.where(first, a, 0.0) for a in couplings]
    couplings = [a.astype(BF16) for a in couplings]
    block = 2
    while block < min(8, size):
        mask = ((rows // block) % 2 == 1) & (cols // block == rows // block - 1)
        inner = [dot(t, a) for t, a in zip(inverses, couplings)]
        inner = [jnp.where(mask, x, 0.0) for x in inner]
        inverses = [t - dot(x, t) for t, x in zip(inverses, inner)]
        block *= 2
    while block < size:
        count = size // (2 * block)
        half_rows = lax.broadcasted_iota(jnp.int32, (size // 2, size), 0)
        half_cols = lax.broadcasted_iota(jnp.int32, (size // 2, size), 1)
        mask = half_cols // block == 2 * (half_rows // block)
        odd = [
            jnp.concatenate(
                [t[(2 * i + 1) * block : (2 * i + 2) * block] for i in range(count)], axis=0
            )
            for t in inverses
        ]
        inner = [jnp.where(mask, dot(o, a), 0.0) for o, a in zip(odd, couplings)]
        odd = [o - dot(x, t) for o, x, t in zip(odd, inner, inverses)]
        inverses = [
            jnp.concatenate(
                [
                    piece
                    for i in range(count)
                    for piece in (
                        t[2 * i * block : (2 * i + 1) * block],
                        o[i * block : (i + 1) * block],
                    )
                ],
                axis=0,
            )
            for t, o in zip(inverses, odd)
        ]
        block *= 2
    return inverses


def core_kernel(first_request, first_head, together, key_heads, later, *refs):
    lengths, places = refs[:2]
    proj, taps, (decay, beta, init_state, grad_out, state_grad) = refs[2:5], refs[5:8], refs[8:13]
    refs = refs[13:]
    if later:
        old_taps, refs = refs[:3], refs[3 + key_heads :]
    grads, grad_taps = refs[:3], refs[3:6]
    grad_decay, grad_beta = refs[6:8]
    sent, (held, sem) = refs[8:-2], refs[-2:]
    step = pl.program_id(0)
    width = init_state.shape[-1]
    size = proj[0].shape[0] // together
    heads = init_state.shape[1]
    group = heads // key_heads
    rows = lax.broadcasted_iota(jnp.int32, (size, size), 0)
    cols = lax.broadcasted_iota(jnp.int32, (size, size), 1)
    wide_rows = lax.broadcasted_iota(jnp.int32, (size, width), 0)
    causal = rows >= cols
    strict = rows > cols
    lower = causal.astype(F32)
    upper = (rows <= cols).astype(F32)
    one = (rows == cols).astype(F32)

    units = [(r, g) for r in range(together) for g in range(key_heads)]
    pairs = [(r, h) for r in range(together) for h in range(heads)]
    unit_of = {(r, h): r * key_heads + h // group for r, h in pairs}
    spans = [slice(r * size, (r + 1) * size) for r in range(together)]
    request = [first_request + step * together + r for r in range(together)]
    length = [lengths[x] for x in request]
    live_row = [
        (lax.broadcasted_iota(jnp.int32, (heads, size), 1) < n).astype(F32) for n in length
    ]
    live_col = [
        (lax.broadcasted_iota(jnp.int32, (size, heads), 0) < n).astype(F32) for n in length
    ]
    live_wide = [(wide_rows < n).astype(F32) for n in length]
    picked = slice(first_head, first_head + heads)
    gate_row = [decay[r, picked, :] * live_row[r] for r in range(together)]
    rate_row = [beta[r, picked, :] * live_row[r] for r in range(together)]
    cum_row = [exact_dot(x, lower, NT) for x in gate_row]
    cum_col = [exact_dot(lower, x, NT) for x in gate_row]
    rate_col = [exact_dot(one, x, NT) for x in rate_row]
    growth_col = [jnp.exp(x) for x in cum_col]

    def prepare(r, kind, index):
        cut = slice(index * width, (index + 1) * width)
        x = proj[kind][spans[r], cut].astype(F32)
        mixed = x * taps[kind][3:4, cut]
        for i in range(3):
            mixed = mixed + shift_down(x, 3 - i, wide_rows) * taps[kind][i : i + 1, cut]
        gate = 1.0 / (1.0 + jnp.exp(-mixed))
        active = mixed * gate
        return active, gate + active * (1.0 - gate)

    def unit(active, factor):
        total = jnp.sum(active * active, axis=-1, keepdims=True) + EPSILON
        scale = factor * lax.rsqrt(total)
        return active * scale, scale, 1.0 / total

    q_in = [prepare(r, 0, g) for r, g in units]
    k_in = [prepare(r, 1, g) for r, g in units]
    v_in = [prepare(r, 2, h) for r, h in pairs]
    q_unit = [unit(x[0], width ** (-0.5)) for x in q_in]
    k_unit = [unit(x[0], 1.0) for x in k_in]
    q_f = [x[0] for x in q_unit]
    k_f = [x[0] for x in k_unit]
    q_b = [x.astype(BF16) for x in q_f]
    k_b = [x.astype(BF16) for x in k_f]
    kk = [dot(k, k, NT) for k in k_b]
    qk = [dot(q, k, NT) for q, k in zip(q_b, k_b)]
    kq = [dot(k, q, NT) for q, k in zip(q_b, k_b)]

    every = range(len(pairs))
    of = [unit_of[p] for p in pairs]
    cum_c = [cum_col[r][:, h : h + 1] for r, h in pairs]
    cum_r = [cum_row[r][h : h + 1, :] for r, h in pairs]
    rate = [rate_col[r][:, h : h + 1] for r, h in pairs]
    growth = [growth_col[r][:, h : h + 1] for r, h in pairs]
    last = [x[:, size - 1 :] for x in cum_r]
    final = [jnp.exp(x) for x in last]
    rest = [jnp.exp(last[i] - cum_c[i]) for i in every]
    within = [jnp.exp(jnp.where(causal, cum_c[i] - cum_r[i], -jnp.inf)) for i in every]
    within_t = [jnp.exp(jnp.where(rows <= cols, cum_r[i] - cum_c[i], -jnp.inf)) for i in every]
    couplings = [jnp.where(strict, rate[i] * kk[of[i]] * within[i], 0.0) for i in every]
    inverses = [t.astype(BF16) for t in unit_lower_inverse(couplings, rows, cols)]

    s_b = [init_state[r, h].astype(BF16) for r, h in pairs]
    ds_b = [state_grad[r, h].astype(BF16) for r, h in pairs]
    k_s = [dot(k_b[of[i]], s_b[i]) for i in every]
    left = [v_in[i][0] - growth[i] * k_s[i] for i in every]
    new_b = [dot(inverses[i], rate[i] * left[i]).astype(BF16) for i in every]
    out_b = [
        (grad_out[spans[r], h * width : (h + 1) * width].astype(F32) * live_wide[r]).astype(BF16)
        for r, h in pairs
    ]
    d_new = [
        dot(kq[of[i]] * within_t[i], out_b[i]) + rest[i] * dot(k_b[of[i]], ds_b[i]) for i in every
    ]
    d_right = [dot(inverses[i], d_new[i], TN) for i in every]
    d_scores = [dot(out_b[i], new_b[i], NT) * within[i] for i in every]
    d_coup = [
        jnp.where(strict, -dot(d_right[i], new_b[i], NT) * within[i], 0.0) for i in every
    ]
    back_b = [(-(rate[i] * growth[i]) * d_right[i]).astype(BF16) for i in every]
    u_q = [growth[i] * dot(out_b[i], s_b[i], NT) for i in every]
    u_k = [dot(back_b[i], s_b[i], NT) for i in every]
    u_e = [rest[i] * dot(new_b[i], ds_b[i], NT) for i in every]

    def leave(r):
        place = places[first_request + step * together + r]
        return [
            pltpu.make_async_copy(
                held.at[r, pl.ds(g * group, group)], sent[g].at[place], sem.at[r, g]
            )
            for g in range(key_heads)
        ]

    @pl.when(step > 0)
    def _():
        for r in range(together):
            for copy in leave(r):
                copy.wait()

    cum_from_rows, cum_from_cols, rate_grads, last_grads = [], [], [], []
    for i, (r, h) in enumerate(pairs):
        u = of[i]
        y = d_coup[i] * kk[u]
        y_row = jnp.sum(y, axis=-1, keepdims=True)
        scored = d_scores[i] * qk[u]
        ended = jnp.sum(k_f[u] * u_e[i], axis=-1, keepdims=True)
        rate_grads.append(jnp.sum(d_right[i] * left[i], axis=-1, keepdims=True) + y_row)
        direct = q_f[u] * u_q[i] + k_f[u] * u_k[i] + scored
        cum_from_rows.append(jnp.sum(direct, axis=-1, keepdims=True) + rate[i] * y_row - ended)
        cum_from_cols.append(jnp.sum(scored + rate[i] * y, axis=0, keepdims=True))
        carried = jnp.sum(state_grad[r, h] * init_state[r, h], axis=0, keepdims=True)
        last_grads.append(
            jnp.sum(ended, axis=0, keepdims=True)
            + final[i] * jnp.sum(carried, axis=1, keepdims=True)
        )
        held[r, h] = (
            final[i] * state_grad[r, h]
            + dot(q_b[u], growth[i] * out_b[i].astype(F32), TN)
            + dot(k_b[u], back_b[i], TN)
        ).astype(BF16)
    for r in range(together):
        for copy in leave(r):
            copy.start()
    for r in range(together):
        mine = [i for i in every if pairs[i][0] == r]
        gate_grad = exact_dot(upper, jnp.concatenate([cum_from_rows[i] for i in mine], axis=1))
        gate_grad = gate_grad - exact_dot(
            upper, jnp.concatenate([cum_from_cols[i] for i in mine], axis=0), NT
        )
        gate_grad = gate_grad + jnp.concatenate([last_grads[i] for i in mine], axis=1)
        grad_decay[spans[r], :] = gate_grad * live_col[r]
        grad_beta[spans[r], :] = (
            jnp.concatenate([rate_grads[i] for i in mine], axis=1) * live_col[r]
        )

    @pl.when(step == 0)
    def _():
        for i, grad_tap in enumerate(grad_taps):
            grad_tap[...] = old_taps[i][...] if later else jnp.zeros_like(grad_tap)

    def conv_back(d_active, slope, r, kind, index):
        cut = slice(index * width, (index + 1) * width)
        x = proj[kind][spans[r], cut].astype(F32)
        d_mixed = d_active * slope
        d_x = d_mixed * taps[kind][3:4, cut]
        sums = []
        for i in range(3):
            moved = shift_up(d_mixed, 3 - i, wide_rows)
            d_x = d_x + moved * taps[kind][i : i + 1, cut]
            sums.append(jnp.sum(moved * x, axis=0, keepdims=True))
        sums.append(jnp.sum(d_mixed * x, axis=0, keepdims=True))
        grads[kind][spans[r], cut] = d_x.astype(BF16)
        grad_taps[kind][:, cut] += jnp.concatenate(sums, axis=0)

    def unit_back(d_unit, unit_in, active):
        unit_rows, scale, inverse_total = unit_in
        inner = jnp.sum(d_unit * active, axis=-1, keepdims=True)
        return scale * (d_unit - active * (inner * inverse_total))

    for u, (r, g) in enumerate(units):
        members = [i for i in every if of[i] == u]
        scores_sum = sum(d_scores[i] for i in members).astype(BF16)
        kk_sum = sum(rate[i] * d_coup[i] for i in members)
        kk_sum = (kk_sum + kk_sum.T).astype(BF16)
        d_q = sum(u_q[i] for i in members) + dot(scores_sum, k_b[u])
        d_k = sum(u_k[i] + u_e[i] for i in members)
        d_k = d_k + dot(scores_sum, q_b[u], TN) + dot(kk_sum, k_b[u])
        conv_back(unit_back(d_q, q_unit[u], q_in[u][0]), q_in[u][1], r, 0, g)
        conv_back(unit_back(d_k, k_unit[u], k_in[u][0]), k_in[u][1], r, 1, g)
    for i, (r, h) in enumerate(pairs):
        conv_back(rate[i] * d_right[i], v_in[i][1], r, 2, h)

    @pl.when(step == pl.num_programs(0) - 1)
    def _():
        for r in range(together):
            for copy in leave(r):
                copy.wait()


def core_call(
    together, first, count, members, proj, taps, decay, beta, init_state, grad_out, state_grad,
    lengths, places, sent_shape, before,
):
    all_heads, width = init_state.shape[1:3]
    size = decay.shape[2]
    key_heads = len(members)
    heads = key_heads * (all_heads * width // proj[0].shape[1])
    part = members[0] // key_heads
    first_head = part * heads
    widths = [key_heads * width, key_heads * width, heads * width]
    rows = count * size
    start = first // together

    def here(offset, column, columns):
        return pl.BlockSpec((together * size, columns), lambda i, *_: (offset + i, column))

    def fixed(array, column, columns):
        return pl.BlockSpec((array.shape[0], columns), lambda i, *_: (0, column))

    by_request = pl.BlockSpec((together, all_heads, size), lambda i, *_: (start + i, 0, 0))
    state = pl.BlockSpec((together, heads, width, width), lambda i, *_: (start + i, part, 0, 0))
    small = pl.BlockSpec((together * size, heads), lambda i, *_: (i, 0))
    anywhere = pl.BlockSpec(memory_space=pl.ANY)
    kept = [] if before is None else [*before[3:6], *[before[8 + g] for g in members]]
    kept_columns = [part if x.shape[1] > n else 0 for x, n in zip(kept, widths)]
    products = count * heads * 26 * 2 * size * width * width
    return pl.pallas_call(
        functools.partial(core_kernel, first, first_head, together, key_heads, bool(kept)),
        grid_spec=pltpu.PrefetchScalarGridSpec(
            num_scalar_prefetch=2,
            grid=(count // together,),
            in_specs=[here(0, part, n) for n in widths]
            + [fixed(x, part, n) for x, n in zip(taps, widths)]
            + [by_request, by_request, state, here(start, part, heads * width), state]
            + [fixed(x, j, n) for x, j, n in zip(kept, kept_columns, widths)]
            + [anywhere] * (key_heads if kept else 0),
            out_specs=[here(0, 0, n) for n in widths]
            + [fixed(x, 0, n) for x, n in zip(taps, widths)]
            + [small, small] + [anywhere] * key_heads,
            scratch_shapes=[
                pltpu.VMEM((together, heads, width, width), BF16),
                pltpu.SemaphoreType.DMA((together, key_heads)),
            ],
        ),
        out_shape=[jax.ShapeDtypeStruct((rows, n), BF16) for n in widths]
        + [jax.ShapeDtypeStruct((x.shape[0], n), F32) for x, n in zip(taps, widths)]
        + [jax.ShapeDtypeStruct((rows, heads), F32)] * 2
        + [jax.ShapeDtypeStruct(sent_shape, BF16)] * key_heads,
        input_output_aliases={16 + g: 8 + g for g in range(key_heads)} if kept else {},
        compiler_params=pltpu.CompilerParams(vmem_limit_bytes=50 << 20),
        cost_estimate=cost(12 * products, count * heads * 400000),
        name="core_grads",
    )(
        lengths, places, *proj, *taps, decay, beta, init_state, grad_out, state_grad, *kept
    )


COST = 10**9
FINISH = 15 * 10**9


def whole(array):
    return pl.BlockSpec(array.shape, lambda *_: (0,) * len(array.shape))


def cost(flops, size):
    return pl.CostEstimate(flops=flops // COST, bytes_accessed=size // COST, transcendentals=0)


def assemble_kernel(indices, own, other, features):
    chips, _, width = own.shape
    for i in range(chips):
        for j, block in enumerate((own, other)):
            start = pl.multiple_of(indices[j * chips + i] * width, width)
            features[:, pl.ds(start, width)] = block[i]


def assemble(indices, blocks):
    chips, rows, width = blocks[0].shape
    tile = 128
    return pl.pallas_call(
        assemble_kernel,
        grid_spec=pltpu.PrefetchScalarGridSpec(
            num_scalar_prefetch=1,
            grid=(rows // tile,),
            in_specs=[pl.BlockSpec((chips, tile, width), lambda i, *_: (0, i, 0))] * 2,
            out_specs=pl.BlockSpec((tile, width * 2 * chips), lambda i, *_: (i, 0)),
        ),
        out_shape=jax.ShapeDtypeStruct((rows, width * 2 * chips), BF16),
        compiler_params=pltpu.CompilerParams(vmem_limit_bytes=32 << 20),
        cost_estimate=cost(1, 4 << 20),
        name="assemble",
    )(indices, *blocks)


def term_kernel(sets, *refs):
    grads, weights, (out, held) = refs[: 3 * sets], refs[3 * sets : 3 * sets + 3], refs[-2:]
    width = out.shape[2]

    @pl.when(pl.program_id(0) == 0)
    def _():
        column = 0
        for kind in range(3):
            for g in range(sets):
                grad = grads[3 * g + kind]
                held[:, column : column + grad.shape[1]] = grad[...]
                column += grad.shape[1]

    total, column = 0.0, 0
    for weight in weights:
        total = total + dot(held[:, column : column + weight.shape[1]], weight[...], NT)
        column += weight.shape[1]
    for i in range(out.shape[0]):
        out[i] = total[:, i * width : (i + 1) * width].astype(BF16)


def head_terms(parts, sets, weights):
    rows = sets[0][0].shape[0]
    depth = weights[0].shape[0]
    columns = sum(w.shape[1] for w in weights)
    width = depth // parts
    tile = max(1, 512 // width)
    grads = [x for group in sets for x in group]
    return pl.pallas_call(
        functools.partial(term_kernel, len(sets)),
        grid=(parts // tile,),
        in_specs=[whole(x) for x in grads]
        + [pl.BlockSpec((tile * width, w.shape[1]), lambda i: (i, 0)) for w in weights],
        out_specs=pl.BlockSpec((tile, rows, width), lambda i: (i, 0, 0)),
        out_shape=jax.ShapeDtypeStruct((parts, rows, width), BF16),
        scratch_shapes=[pltpu.VMEM((rows, columns), BF16)],
        compiler_params=pltpu.CompilerParams(vmem_limit_bytes=50 << 20),
        cost_estimate=cost(2 * rows * depth * columns, 7 << 20),
        name="head_terms",
    )(*grads, *weights)


def weight_kernel(parts, chunks, plan, order, *refs):
    features, grads = refs[:chunks], refs[chunks : 4 * chunks]
    taps, states = refs[4 * chunks : 4 * chunks + 3], refs[4 * chunks + 3]
    outs, turned = refs[4 * chunks + 4 : -1], refs[-1]
    step = pl.program_id(0)
    starts = [sum(x.shape[0] for x in features[:i]) for i in range(chunks)]
    width = states.shape[2]

    @pl.when(step == 0)
    def _():
        for c, start in enumerate(starts):
            row = 0
            for grad in grads[3 * c : 3 * c + 3]:
                count, columns = grad.shape
                turned[row : row + columns, start : start + count] = grad[...].T
                row += columns
        for index, row, hop in plan["states"]:
            for t in range(states.shape[0] // parts * states.shape[1]):
                slot, head = divmod(t, states.shape[1])
                tall, wide = divmod(t, outs[index].shape[1] // width)
                outs[index][
                    row + tall * width : row + (tall + 1) * width, wide * width : (wide + 1) * width
                ] = states[hop * (states.shape[0] // parts) + slot, head]
        for index, row in plan["taps"]:
            store_taps(outs[index], row, tap_pieces(taps, width))

    total = sum(
        dot(turned[:, start : start + x.shape[0]], x[...]) for start, x in zip(starts, features)
    )
    for hop, pieces in plan["weights"]:

        @pl.when(step == plan["hops"].index(hop))
        def _():
            for index, row, low, high in pieces:
                outs[index][row : row + high - low, :] = total[low:high].astype(outs[index].dtype)


def tap_pieces(taps, width):
    return [x[:, i * width : (i + 1) * width] for x in taps for i in range(x.shape[1] // width)]


def store_taps(out, row, pieces):
    width = pieces[0].shape[1]
    across = out.shape[1] // width
    for index, piece in enumerate(pieces):
        high = piece.astype(BF16).astype(F32)
        block = jnp.concatenate([high, piece - high], axis=0)
        block = jnp.concatenate([block, jnp.zeros_like(block)], axis=0).astype(BF16)
        start = row + index // across * 16
        out[start : start + 16, index % across * width : (index % across + 1) * width] = block


def load_taps(source, row, count, width):
    across = source.shape[1] // width
    pieces = []
    for index in range(count):
        start = row + index // across * 16
        block = source[start : start + 16, index % across * width : (index % across + 1) * width]
        block = block.astype(F32)
        pieces.append(block[:4] + block[4:8])
    return pieces


def rounded_taps(pieces):
    highs = [piece.astype(BF16).astype(F32) for piece in pieces]
    return [high + (piece - high).astype(BF16).astype(F32) for piece, high in zip(pieces, highs)]


def weight_plan(parts, columns, depth, states, pieces):
    width = states.shape[2]
    tiles = states.shape[0] // parts * states.shape[1]
    state_rows = -(-tiles // (depth // width)) * width
    tap_rows = -(-pieces // (depth // width)) * 16
    if parts == 4:
        half = columns // 2
        plan = {
            "hops": [3, 1, 2, 0],
            "weights": [
                (3, [(0, half, 0, half), (1, half, half, columns)]),
                (1, [(0, 0, 0, half), (3, 0, half, columns)]),
                (2, [(1, 0, half, columns), (2, 0, 0, half)]),
                (0, [(4, 0, 0, columns)]),
            ],
            "states": [
                (0, columns, 1), (0, columns + state_rows, 3), (1, columns, 2),
            ],
            "taps": [(0, columns + 2 * state_rows)],
        }
        shapes = [
            ((columns + 2 * state_rows + tap_rows, depth), BF16),
            ((columns + state_rows, depth), BF16),
            ((half, depth), F32),
            ((half, depth), F32),
            ((columns, depth), F32),
        ]
    else:
        hops = [*range(1, parts), 0]
        plan = {
            "hops": hops,
            "weights": [(hop, [(i, 0, 0, columns)]) for i, hop in enumerate(hops)],
            "states": [(i, columns, hop) for i, hop in enumerate(hops[:-1])],
            "taps": [(i, columns + state_rows) for i in range(parts - 1)],
        }
        shapes = [((columns + state_rows + tap_rows, depth), BF16)] * (parts - 1)
        shapes.append(((columns, depth), F32))
    return plan, [jax.ShapeDtypeStruct(*x) for x in shapes], state_rows, tap_rows


def weight_blocks(me, parts, plan, shapes, features, grads, index, widths, taps, states):
    depth = features[0].shape[1] // parts
    columns = sum(widths)
    rows = sum(x.shape[0] for x in features)
    order = jnp.bitwise_xor(me, jnp.array(plan["hops"], jnp.int32))

    def of_key_head(array, width):
        place = index if array.shape[1] > width else 0
        return pl.BlockSpec((array.shape[0], width), lambda i, order: (0, place))

    return pl.pallas_call(
        functools.partial(weight_kernel, parts, len(features), plan),
        grid_spec=pltpu.PrefetchScalarGridSpec(
            num_scalar_prefetch=1,
            grid=(parts,),
            in_specs=[
                pl.BlockSpec((x.shape[0], depth), lambda i, order: (0, order[i]))
                for x in features
            ]
            + [of_key_head(x, n) for group in grads for x, n in zip(group, widths)]
            + [whole(x) for x in (*taps, states)],
            out_specs=[whole(x) for x in shapes],
            scratch_shapes=[pltpu.VMEM((columns, rows), BF16)],
        ),
        out_shape=shapes,
        compiler_params=pltpu.CompilerParams(vmem_limit_bytes=50 << 20),
        cost_estimate=cost(2 * rows * depth * parts * columns, 8 << 20),
        name="weight_blocks",
    )(order, *features, *[x for group in grads for x in group], *taps, states)


def middle_kernel(half, state_rows, *refs):
    first, second, kept_first, kept_second = refs[:4]
    taps, (next_first, next_second) = refs[4:7], refs[7:]
    columns, width = 2 * half, taps[0].shape[1]
    next_first[:half, :] = (kept_first[...] + first[half:columns, :].astype(F32)).astype(BF16)
    next_second[...] = (kept_second[...] + second[half:columns, :].astype(F32)).astype(BF16)
    start = columns + state_rows
    next_first[half : half + state_rows, :] = first[start : start + state_rows, :]
    mine = rounded_taps(tap_pieces(taps, width))
    theirs = load_taps(first, columns + 2 * state_rows, len(mine), width)
    store_taps(next_first, half + state_rows, [a + b for a, b in zip(mine, theirs)])


def exchange(arrays, taps, parts, columns, state_rows, tap_rows):
    if parts != 4:
        return [swap(x, "batch", parts, hop + 1) for hop, x in enumerate(arrays[:-1])]
    half, depth = columns // 2, arrays[0].shape[1]
    first, second = swap(arrays[0], "batch", parts, 1), swap(arrays[1], "batch", parts, 2)
    shapes = [
        jax.ShapeDtypeStruct((half + state_rows + tap_rows, depth), BF16),
        jax.ShapeDtypeStruct((half, depth), BF16),
    ]
    inputs = [first, second, arrays[2], arrays[3], *taps]
    next_first, next_second = pl.pallas_call(
        functools.partial(middle_kernel, half, state_rows),
        grid=(1,),
        in_specs=[whole(x) for x in inputs],
        out_specs=[whole(x) for x in shapes],
        out_shape=shapes,
        compiler_params=pltpu.CompilerParams(vmem_limit_bytes=40 << 20),
        cost_estimate=cost(1, 1),
        name="pass_on",
    )(*inputs)
    return [first, second, next_first, next_second]


def second_exchange(arrays, parts):
    if parts != 4:
        return arrays
    return [*arrays[:2], swap(arrays[2], "batch", parts, 2), swap(arrays[3], "batch", parts, 1)]


def finish_kernel(parts, key_heads, widths, sources, ranks, *refs):
    hidden_parts, joined, refs = refs[:2], refs[-1], refs[2:-1]
    columns, half = sum(widths), sum(widths) // 2
    taps, kept, refs = refs[: 3 * key_heads], refs[3 * key_heads : 4 * key_heads], refs[4 * key_heads :]
    outs, out, tap_outs = refs[-7:-4], refs[-4], refs[-3:]
    refs = refs[:-7]
    per = len(refs) // key_heads
    count = 4 if parts == 4 else parts - 1
    hops = parts - 1
    group, width = kept[0].shape[1], kept[0].shape[2]
    step = pl.program_id(0)
    for g in range(key_heads):
        own, *rest = refs[g * per : (g + 1) * per]
        pieces, states, edges = rest[:count], rest[count : count + hops], rest[count + hops :]
        if parts == 4:
            upper = own[:half] + (pieces[0][...].astype(F32) + pieces[2][...].astype(F32))
            lower = own[half:] + (pieces[1][...].astype(F32) + pieces[3][...].astype(F32))
            total = jnp.concatenate([upper.T, lower.T], axis=1)
        else:
            total = sum((piece[...].astype(F32) for piece in pieces), own[...]).T
        start = 0
        for weight, size in zip(outs, widths):
            weight[:, g * size : (g + 1) * size] = total[:, start : start + size]
            start += size
        across = states[0].shape[1] // width
        for j in range(out.shape[0]):
            source, rank = sources[step * out.shape[0] + j], ranks[step * out.shape[0] + j]

            @pl.when(source == 0)
            def _():
                out[j, g * group : (g + 1) * group] = kept[g][rank].astype(F32)

            for hop, block in enumerate(states):
                for slot in range(kept[g].shape[0]):

                    @pl.when((source == hop + 1) & (rank == slot))
                    def _():
                        for h in range(group):
                            tall, wide = divmod(slot * group + h, across)
                            out[j, g * group + h] = block[
                                tall * width : (tall + 1) * width, wide * width : (wide + 1) * width
                            ].astype(F32)

        @pl.when(step == 0)
        def _():
            count = hidden_parts[0].shape[0]
            joined[:count, :] = hidden_parts[0][...]
            joined[count:, :] = hidden_parts[1][...]
            mine = rounded_taps(tap_pieces(taps[3 * g : 3 * g + 3], width))
            others = [load_taps(x, 0, len(mine), width) for x in edges]
            if parts == 4:
                mine = rounded_taps([a + b for a, b in zip(mine, others.pop(0))])
            groups = [mine, *others]
            while len(groups) > 1:
                groups = [
                    [a + b for a, b in zip(groups[i], groups[i + 1])]
                    for i in range(0, len(groups), 2)
                ]
            sums = groups[0]
            for tap_out in tap_outs:
                size = tap_out.shape[1] // key_heads
                for i in range(size // width):
                    start = g * size + i * width
                    tap_out[:, start : start + width] = sums.pop(0)


def finish(parts, sources, ranks, hidden_rows, taps, sent, own, pieces, widths, state_rows, tap_rows):
    requests, key_heads = sources.shape[0], len(sent)
    columns, rows = sum(widths), own[0].shape[1]
    group, width = sent[0].shape[1:3]
    capacity = sent[0].shape[0] // parts
    tile = min(rows, 128)
    tiles = rows // tile
    together = requests // tiles
    if parts == 4:
        state_places = [(0, columns), (1, columns), (2, columns // 2)]
        tap_places = [(0, columns + 2 * state_rows), (2, columns // 2 + state_rows)]
    else:
        state_places = [(i, columns) for i in range(parts - 1)]
        tap_places = [(i, columns + state_rows) for i in range(parts - 1)]

    def rows_at(start, count):
        return pl.BlockSpec((count, rows), lambda i, *_: (start // count, 0))

    def column(count):
        return pl.BlockSpec((count, tile), lambda i, *_: (0, i))

    inputs, specs = [], []
    for mine, group_pieces in zip(own, pieces):
        inputs += [mine, *group_pieces]
        specs += [column(columns)]
        specs += [column(columns // 2 if parts == 4 else columns)] * len(group_pieces)
        inputs += [group_pieces[i] for i, _ in (*state_places, *tap_places)]
        specs += [rows_at(start, state_rows) for _, start in state_places]
        specs += [rows_at(start, tap_rows) for _, start in tap_places]
    sizes = [key_heads * n for n in widths]
    heads = key_heads * group
    joined = jax.ShapeDtypeStruct(
        (sum(x.shape[0] for x in hidden_rows), hidden_rows[0].shape[1]), BF16
    )
    return pl.pallas_call(
        functools.partial(finish_kernel, parts, key_heads, widths),
        grid_spec=pltpu.PrefetchScalarGridSpec(
            num_scalar_prefetch=2,
            grid=(tiles,),
            in_specs=[whole(x) for x in (*hidden_rows, *taps)]
            + [pl.BlockSpec((capacity, group, width, width), lambda i, *_: (0, 0, 0, 0))] * key_heads
            + specs,
            out_specs=[pl.BlockSpec((tile, n), lambda i, *_: (i, 0)) for n in sizes]
            + [pl.BlockSpec((together, heads, width, width), lambda i, *_: (i, 0, 0, 0))]
            + [pl.BlockSpec((taps[0].shape[0], n), lambda i, *_: (0, 0)) for n in sizes]
            + [whole(joined)],
        ),
        out_shape=[jax.ShapeDtypeStruct((rows, n), F32) for n in sizes]
        + [jax.ShapeDtypeStruct((requests, heads, width, width), F32)]
        + [jax.ShapeDtypeStruct((taps[0].shape[0], n), F32) for n in sizes]
        + [joined],
        compiler_params=pltpu.CompilerParams(vmem_limit_bytes=50 << 20),
        cost_estimate=pl.CostEstimate(flops=FINISH, bytes_accessed=1, transcendentals=0),
        name="finish",
    )(sources, ranks, *hidden_rows, *taps, *sent, *inputs)


def slot_plan(slot_map, all_slots, me, parts):
    requests = slot_map.shape[0]
    capacity = max(1, requests // parts)
    owners = all_slots // requests
    request_ids = jnp.arange(all_slots.shape[0], dtype=jnp.int32)
    earlier = (
        (request_ids[:, None] > request_ids[None, :])
        & (request_ids[:, None] // requests == request_ids[None, :] // requests)
        & (owners[:, None] == owners[None, :])
    )
    ranks = jnp.sum(earlier.astype(jnp.int32), axis=1)
    hops = jnp.bitwise_xor(owners, request_ids // requests)
    places = lax.dynamic_slice_in_dim(hops * capacity + ranks, me * requests, requests)
    own_slots = me * requests + jnp.arange(requests, dtype=jnp.int32)
    matches = (all_slots[None, :] == own_slots[:, None]).astype(jnp.int32)
    sources = jnp.sum(matches * hops[None, :], axis=1)
    source_ranks = jnp.sum(matches * ranks[None, :], axis=1)
    return places, sources, source_ranks, capacity


def swap(array, axis, parts, hop):
    return lax.ppermute(array, axis, [(i, i ^ hop) for i in range(parts)])


def along(array, parts, hop):
    chips = parts // 2
    pairs = [(2 * z + c, 2 * ((z + hop) % chips) + c) for z in range(chips) for c in range(2)]
    return lax.ppermute(array, "tensor", pairs)


def body(
    hidden, w_query, w_key, w_value, conv_query, conv_key, conv_value, decay_log, beta_gate,
    init_state, grad_out, state_grad_in, rollout_lengths, slot_map,
):
    parts, spread = lax.axis_size("batch"), lax.axis_size("tensor")
    chips = spread // 2
    me, mine = lax.axis_index("batch"), lax.axis_index("tensor")
    chip, core = mine // 2, mine % 2
    requests = rollout_lengths.shape[0]
    size = hidden.shape[0] // requests
    heads, width = init_state.shape[1], init_state.shape[2]
    chunks = [requests // 2, requests - requests // 2]
    starts = [sum(chunks[:i]) for i in range(len(chunks))]

    shard = hidden[: chunks[0] * size]
    rest = hidden[chunks[0] * size :]
    blocks = [shard] + [along(shard, spread, hop) for hop in range(1, chips)]
    all_slots = lax.all_gather(slot_map, "batch", axis=0, tiled=True)
    places, sources, ranks, capacity = slot_plan(slot_map, all_slots, me, parts)
    rest, blocks, places, sources, ranks = lax.optimization_barrier(
        (rest, blocks, places, sources, ranks)
    )
    blocks = jnp.stack(blocks)
    blocks = [blocks, swap(blocks, "tensor", spread, 1)]
    chip_steps = jnp.arange(chips, dtype=jnp.int32)
    came = (chip - chip_steps) % chips * 2
    indices = jnp.concatenate([came + core, came + 1 - core])
    gathered = [
        assemble(indices, blocks), lax.all_gather(rest, "tensor", axis=1, tiled=True),
    ]

    def by_head(array):
        return array.reshape(requests, size, heads).transpose(0, 2, 1)

    taps = [conv_query, conv_key, conv_value]
    weights = [w_query, w_key, w_value]
    key_heads = w_query.shape[1] // width
    group = heads // key_heads
    sent_shape = (parts * capacity, group, width, width)
    widths = (width, width, group * width)
    out, hidden_rows, own, pieces, decays, betas, sent = None, [], [], [], [], [], None
    for i, (start, count) in enumerate(zip(starts, chunks)):
        proj = [
            jnp.dot(gathered[i], w, preferred_element_type=F32).astype(BF16) for w in weights
        ]
        last = i == len(chunks) - 1
        sets = [range(g, g + 1) for g in range(key_heads)] if last else [range(key_heads)]
        grads, tap_sums, chunk_decays, chunk_betas = [], [], [], []
        earlier = out
        for members in sets:
            together = max(
                n for n in (1, 2, 4)
                if n * len(members) <= 4 and count % n == 0 and start % n == 0
            )
            before = earlier
            out = core_call(
                together, start, count, members, proj, taps, by_head(decay_log),
                by_head(beta_gate), init_state, grad_out, state_grad_in, rollout_lengths,
                places, sent_shape, before,
            )
            grads.append(out[:3])
            tap_sums += out[3:6]
            chunk_decays.append(out[6])
            chunk_betas.append(out[7])
            if last:
                g = members[0]
                if g == key_heads - 1:
                    term = head_terms(spread, grads, weights)
                    term, out, pieces = lax.optimization_barrier((term, out, pieces))
                states = jax.ShapeDtypeStruct(sent_shape, BF16)
                plan, shapes, state_rows, tap_rows = weight_plan(
                    parts, sum(widths), gathered[0].shape[1] // parts, states,
                    sum(widths) // width,
                )
                local = weight_blocks(
                    me, parts, plan, shapes, gathered, [earlier[:3], out[:3]], g, widths,
                    out[3:6], out[8],
                )
                if g < key_heads - 1:
                    local, proj = lax.optimization_barrier((local, proj))
                own.append(local[-1])
                pieces.append(
                    exchange(local, out[3:6], parts, sum(widths), state_rows, tap_rows)
                )
                sent = [*(sent or []), out[8]]
            elif members[-1] == key_heads - 1:
                term = head_terms(spread, grads, weights)
        decays.append(jnp.concatenate(chunk_decays, axis=1))
        betas.append(jnp.concatenate(chunk_betas, axis=1))
        term = term.reshape(-1, term.shape[2])
        hidden_rows.append(lax.psum_scatter(term, "tensor", scatter_dimension=0, tiled=True))
    pieces = [second_exchange(x, parts) for x in pieces]
    *grad_w, slot_state_grad, tap_q, tap_k, tap_v, grad_hidden = finish(
        parts, sources, ranks, hidden_rows, tap_sums, sent, own, pieces, widths, state_rows, tap_rows
    )
    return (
        grad_hidden, *grad_w, tap_q, tap_k, tap_v, jnp.concatenate(decays), jnp.concatenate(betas),
        slot_state_grad,
    )


def solution(mesh):
    placed = (
        P("batch", "tensor"),
        P(None, "tensor"),
        P(None, "tensor"),
        P(None, "tensor"),
        P(None, "tensor"),
        P(None, "tensor"),
        P(None, "tensor"),
        P("batch", "tensor"),
        P("batch", "tensor"),
        P("batch", "tensor", None, None),
        P("batch", "tensor"),
        P("batch", "tensor", None, None),
        P("batch"),
        P("batch"),
    )
    return jax.shard_map(
        body,
        mesh=mesh,
        in_specs=placed,
        out_specs=(
            P("batch", "tensor"),
            P("batch", "tensor"),
            P("batch", "tensor"),
            P("batch", "tensor"),
            P(None, "tensor"),
            P(None, "tensor"),
            P(None, "tensor"),
            P("batch", "tensor"),
            P("batch", "tensor"),
            P("batch", "tensor", None, None),
        ),
        check_vma=False,
    )
```
